512 devices in a mesh: gy: 4 (over z_hi, core), gx: 4 (over z_lo), dp: 32 (over x, y).
Axes of the slice: x: 4, y: 8, z: 8 (z_hi: 2, z_lo: 4; z = z_hi * 4 + z_lo), core: 2. Of those that a mesh axis runs over, the one named last changes fastest.
Arguments:
- tokens: bfloat16 [32, 4, 4, 128, 512], P('dp', 'gy', 'gx'), may hold values from -6 to 6
- tile_ids: int32 [32, 4, 4, 2], P('dp'), may hold values from -1 to 15, as said below
- w_qkv: bfloat16 [512, 768], P('dp'), may hold values from -0.25 to 0.25
- w_out: bfloat16 [256, 512], P('dp'), may hold values from -0.75 to 0.75
- norm_gain: float32 [512], replicated, may hold values from 0.1 to 1.9
- rel_bias: float32 [8, 49], replicated, may hold values from -2 to 304
- update_grad: bfloat16 [32, 4, 4, 128, 512], P('dp', 'gy', 'gx'), may hold values from -6 to 6
Outputs:
- update: bfloat16 [32, 4, 4, 128, 512], P('dp', 'gy', 'gx')
- grad_tokens: bfloat16 [32, 4, 4, 128, 512], P('dp', 'gy', 'gx')
- grad_qkv: float32 [512, 768], P('dp')
- grad_out: float32 [256, 512], P('dp')
- grad_gain: float32 [512], replicated
- grad_bias: float32 [8, 49], replicated
The draws below stay inside these ranges and needn't reach their ends.
Inputs may be any that keep to these rules, and one draw needn't show every extreme that they name: `tile_ids`: for each crop and device the slots first hold distinct tiles of that device's region, numbered row by row with 4 to a row, then -1; each device lists exactly 2 tiles, so no slot holds -1.
All inputs are finite; a program needn't handle non-finite values.
Results may differ from the reference program's by a relative error of at most 0.027.
Values may be sent and summed in bfloat16 or wider, within the bound.
No kernel may reach another device: no remote copies, remote signals or barrier semaphores. Data moves between devices by JAX's collectives and lax.ppermute only.
A program may use at most 64 MiB of HBM per device.

```python
import jax
import jax.numpy as jnp
from jax import lax

D = 512
HEADS = 8
HD = 32
INNER = 256
TILE = 8
WIN = 7
HALO = 3
REG = 4
CAP = 2
ROWS = 128
CROPS = 32
N_GY = 4
N_GX = 4


def draw_tile_ids(key, part):
    keys_all = jax.random.split(key, 5)
    devices = N_GY * N_GX
    tiles_per = REG * REG
    tile_counts = jax.random.randint(keys_all[0], (CROPS, devices), 2, CAP + 1)
    full_device = jax.random.randint(keys_all[1], (CROPS, 1), 0, devices)
    device_index = jnp.arange(devices, dtype=jnp.int32)
    tile_counts = jnp.where(device_index[None, :] == full_device, CAP, tile_counts)
    centre_row = jax.random.randint(keys_all[2], (CROPS, 1, 1), 0, N_GY * REG)
    centre_col = jax.random.randint(keys_all[3], (CROPS, 1, 1), 0, N_GX * REG)
    local_tile = jnp.arange(tiles_per, dtype=jnp.int32)
    grid_row = (device_index // N_GX)[:, None] * REG + (local_tile // REG)[None, :]
    grid_col = (device_index % N_GX)[:, None] * REG + (local_tile % REG)[None, :]
    distance = (grid_row[None] - centre_row) ** 2 + (grid_col[None] - centre_col) ** 2
    jitter = jax.random.randint(keys_all[4], (CROPS, devices, tiles_per), 0, 4 * tiles_per)
    ranking = (distance + jitter) * tiles_per + local_tile[None, None, :]
    chosen = jnp.argsort(ranking, axis=-1)[:, :, :CAP].astype(jnp.int32)
    slot_number = jnp.arange(CAP, dtype=jnp.int32)[None, None, :]
    listed = jnp.where(slot_number < tile_counts[:, :, None], chosen, -1)
    return listed.reshape(CROPS, N_GY, N_GX, CAP).astype(jnp.int32)


def draw_rel_bias(key, part):
    base_key = jax.random.fold_in(key, 0)
    bias_rows = jax.random.uniform(base_key, (HEADS, WIN * WIN), jnp.float32, -2.0, 2.0)
    return bias_rows.astype(jnp.float32)


def block_scale(key, dims, cuts, least, largest):
    level, own = 1.0, jax.random.fold_in(key, 6)
    for position, blocks in cuts:
        steps = jnp.exp(jax.random.uniform(jax.random.fold_in(own, position), (blocks,), jnp.float32, least / len(cuts), largest / len(cuts)))
        level = level * jnp.repeat(steps, dims[position] // blocks).reshape([-1 if axis == position else 1 for axis in range(len(dims))])
    return level


def scatter_about(rng, shape, spread, most, shards=(), held_as=jnp.bfloat16):
    gain = block_scale(rng, shape, shards, -0.22, 0.18) if shards else 1.0
    drawn = jax.random.normal(rng, shape, jnp.float32) * spread * gain
    return jnp.minimum(jnp.maximum(drawn, -most), most).astype(held_as)


def setup_inputs(seed: int = 0) -> dict:
    key_list = jax.random.split(jax.random.key(seed), 8)
    tokens = scatter_about(key_list[0], (CROPS, N_GY, N_GX, ROWS, D), 1.0, 6.0, ((0, 32), (1, 4), (2, 4)))
    tile_ids = draw_tile_ids(jax.random.fold_in(key_list[7], 71), 0)
    w_qkv = scatter_about(key_list[2], (D, 3 * INNER), D ** -0.5, 0.25, ((0, 32),))
    w_out = scatter_about(key_list[3], (INNER, D), (INNER // 4) ** -0.5, 0.75, ((0, 32),))
    norm_gain = jnp.clip(1.0 + 0.18 * jax.random.normal(key_list[4], (D,), jnp.float32), 0.1, 1.9)
    rel_bias = draw_rel_bias(jax.random.fold_in(key_list[7], 71), 0)
    update_grad = scatter_about(key_list[6], (CROPS, N_GY, N_GX, ROWS, D), 1.0, 6.0, ((0, 32), (1, 4), (2, 4)))
    return {"tokens": tokens, "tile_ids": tile_ids, "w_qkv": w_qkv, "w_out": w_out, "norm_gain": norm_gain, "rel_bias": rel_bias, "update_grad": update_grad}


def window_tables():
    win_side = TILE + 2 * HALO
    query_cells = jnp.arange(TILE * TILE, dtype=jnp.int32)
    window_cells = jnp.arange(win_side * win_side, dtype=jnp.int32)
    row_step = (window_cells // win_side)[None, :] - HALO - (query_cells // TILE)[:, None]
    col_step = (window_cells % win_side)[None, :] - HALO - (query_cells % TILE)[:, None]
    inside = (jnp.abs(row_step) <= HALO) & (jnp.abs(col_step) <= HALO)
    offset = (row_step + HALO) * WIN + col_step + HALO
    onehot = ((offset[None, :, :] == jnp.arange(WIN * WIN, dtype=jnp.int32)[:, None, None]) & inside[None, :, :]).astype(jnp.float32)
    return (inside, onehot)

def softmax_scores(queries, key_rows, bias_table, allowed):
    scores = jnp.einsum('nqhd,nkhd->nhqk', queries.astype(jnp.float32), key_rows.astype(jnp.float32)) * HD ** (-0.5) + bias_table[None]
    scores = jnp.where(allowed, scores, -jnp.inf)
    row_max = lax.optimization_barrier(jnp.max(scores, axis=-1, keepdims=True))
    exponent = jnp.exp(scores - row_max)
    return exponent / lax.optimization_barrier(jnp.sum(exponent, axis=-1, keepdims=True))

def crop_math(crop_tokens, crop_tiles, crop_grad, w_qkv, w_out, norm_gain, bias_table, inside):
    win_side = TILE + 2 * HALO
    win_cells = win_side * win_side
    grid_rows = N_GY * REG
    grid_cols = N_GX * REG
    slot_count = N_GY * N_GX * CAP
    features = crop_tokens.reshape(slot_count * TILE * TILE, D).astype(jnp.float32)
    inv_rms = lax.rsqrt(lax.optimization_barrier(jnp.mean(features * features, axis=-1, keepdims=True)) + 1e-06)
    normed = (features * inv_rms * norm_gain).astype(jnp.bfloat16)
    qkv_rows = jnp.dot(normed, w_qkv, preferred_element_type=jnp.float32).astype(jnp.bfloat16)
    slot_tiles = crop_tiles.reshape(slot_count)
    is_active = slot_tiles >= 0
    tile_index = jnp.where(is_active, slot_tiles, 0)
    slot_number = jnp.arange(slot_count, dtype=jnp.int32)
    dev_row = slot_number // (N_GX * CAP)
    dev_col = slot_number // CAP % N_GX
    tile_row = dev_row * REG + tile_index // REG
    tile_col = dev_col * REG + tile_index % REG
    spare_tile = grid_rows * grid_cols
    flat_tiles = jnp.where(is_active, tile_row * grid_cols + tile_col, spare_tile)
    kv_tiles = qkv_rows[:, INNER:].reshape(slot_count, TILE * TILE, 2 * INNER)
    tile_grid = jnp.zeros((spare_tile + 1, TILE * TILE, 2 * INNER), jnp.bfloat16).at[flat_tiles].set(kv_tiles)[:spare_tile]
    kv_crop = tile_grid.reshape(grid_rows, grid_cols, TILE, TILE, 2 * INNER).transpose(0, 2, 1, 3, 4).reshape(grid_rows * TILE, grid_cols * TILE, 2 * INNER)
    kv_padded = jnp.pad(kv_crop, ((HALO, HALO), (HALO, HALO), (0, 0)))
    crop_active = jnp.zeros((spare_tile + 1,), jnp.float32).at[flat_tiles].set(1.0)[:spare_tile].reshape(grid_rows, grid_cols)
    cell_active = jnp.repeat(jnp.repeat(crop_active, TILE, axis=0), TILE, axis=1)
    key_active = jnp.pad(cell_active, HALO) > 0.5
    start_rows = (tile_row * TILE).astype(jnp.int32)
    start_cols = (tile_col * TILE).astype(jnp.int32)
    zero_index = jnp.zeros((), jnp.int32)
    kv_windows = jax.vmap(lambda first_row, first_col: lax.dynamic_slice(kv_padded, (first_row, first_col, zero_index), (win_side, win_side, 2 * INNER)))(start_rows, start_cols).reshape(slot_count, win_cells, 2 * INNER)
    key_windows = jax.vmap(lambda first_row, first_col: lax.dynamic_slice(key_active, (first_row, first_col), (win_side, win_side)))(start_rows, start_cols).reshape(slot_count, win_cells)
    queries = qkv_rows[:, :INNER].reshape(slot_count, TILE * TILE, HEADS, HD)
    key_rows = kv_windows[:, :, :INNER].reshape(slot_count, win_cells, HEADS, HD)
    values = kv_windows[:, :, INNER:].reshape(slot_count, win_cells, HEADS, HD)
    allowed = inside[None, None] & (key_windows[:, None, None, :] | ~is_active[:, None, None, None])
    attn_probs = softmax_scores(queries, key_rows, bias_table, allowed)
    probs_bf = lax.optimization_barrier(attn_probs.astype(jnp.bfloat16))
    probs_back = probs_bf.astype(jnp.float32)
    attended = jnp.einsum('nhqk,nkhd->nqhd', probs_back, values.astype(jnp.float32)) * is_active[:, None, None, None]
    attended = attended.astype(jnp.bfloat16).reshape(slot_count * TILE * TILE, INNER)
    update = jnp.dot(attended, w_out, preferred_element_type=jnp.float32).astype(jnp.bfloat16)
    row_active = jnp.repeat(is_active, TILE * TILE)
    grad_rows = jnp.where(row_active[:, None], crop_grad.reshape(slot_count * TILE * TILE, D), jnp.zeros((), jnp.bfloat16))
    grad_attended = jnp.dot(grad_rows, w_out.T, preferred_element_type=jnp.float32).astype(jnp.bfloat16)
    grad_out = jnp.dot(attended.T, grad_rows, preferred_element_type=jnp.float32)
    grad_heads = grad_attended.reshape(slot_count, TILE * TILE, HEADS, HD).astype(jnp.float32)
    d_probs = jnp.einsum('nqhd,nkhd->nhqk', grad_heads, values.astype(jnp.float32))
    row_delta = lax.optimization_barrier(jnp.sum(attn_probs * d_probs, axis=-1, keepdims=True))
    d_scores_bf = lax.optimization_barrier((attn_probs * (d_probs - row_delta)).astype(jnp.bfloat16))
    d_scores = d_scores_bf.astype(jnp.float32)
    d_queries = jnp.einsum('nhqk,nkhd->nqhd', d_scores, key_rows.astype(jnp.float32)) * HD ** (-0.5)
    d_keys = jnp.einsum('nhqk,nqhd->nkhd', d_scores, queries.astype(jnp.float32)) * HD ** (-0.5)
    d_values = jnp.einsum('nhqk,nqhd->nkhd', probs_back, grad_heads)
    grad_bias_sum = lax.optimization_barrier(jnp.sum(d_scores, axis=0))
    d_kv_windows = jnp.concatenate([d_keys.reshape(slot_count, win_cells, INNER), d_values.reshape(slot_count, win_cells, INNER)], axis=-1)
    pad_rows = grid_rows * TILE + 2 * HALO
    pad_cols = grid_cols * TILE + 2 * HALO
    cell_index = jnp.arange(win_cells, dtype=jnp.int32)
    targets = (start_rows[:, None] + cell_index[None, :] // win_side) * pad_cols + start_cols[:, None] + cell_index[None, :] % win_side
    grad_padded = jnp.zeros((pad_rows * pad_cols, 2 * INNER), jnp.float32).at[targets.reshape(-1)].add(d_kv_windows.reshape(slot_count * win_cells, 2 * INNER)).reshape(pad_rows, pad_cols, 2 * INNER)
    grad_crop = grad_padded[HALO:HALO + grid_rows * TILE, HALO:HALO + grid_cols * TILE]
    grad_tiles = grad_crop.reshape(grid_rows, TILE, grid_cols, TILE, 2 * INNER).transpose(0, 2, 1, 3, 4).reshape(grid_rows * grid_cols, TILE * TILE, 2 * INNER)
    grad_slots = jnp.where(is_active[:, None, None], grad_tiles[jnp.where(is_active, flat_tiles, 0)], 0.0)
    grad_qkv_rows = jnp.concatenate([d_queries.reshape(slot_count * TILE * TILE, INNER), grad_slots.reshape(slot_count * TILE * TILE, 2 * INNER)], axis=-1).astype(jnp.bfloat16)
    grad_qkv = jnp.dot(normed.T, grad_qkv_rows, preferred_element_type=jnp.float32)
    grad_normed = jnp.dot(grad_qkv_rows, w_qkv.T, preferred_element_type=jnp.float32)
    scaled_grad = grad_normed * norm_gain
    grad_gain = lax.optimization_barrier(jnp.sum(grad_normed * features * inv_rms, axis=0))
    grad_tokens = (inv_rms * scaled_grad - features * inv_rms ** 3 * lax.optimization_barrier(jnp.mean(scaled_grad * features, axis=-1, keepdims=True))).astype(jnp.bfloat16)
    return (update.reshape(crop_tokens.shape), grad_tokens.reshape(crop_tokens.shape), grad_qkv, grad_out, grad_gain, grad_bias_sum)

def reference(tokens, tile_ids, w_qkv, w_out, norm_gain, rel_bias, update_grad):
    inside, onehot = window_tables()
    bias_table = jnp.einsum('ho,oqk->hqk', rel_bias, onehot, precision=lax.Precision.HIGHEST)

    def crop_pass(crop_items):
        crop_tokens, crop_tiles, crop_grad = crop_items
        return crop_math(crop_tokens, crop_tiles, crop_grad, w_qkv, w_out, norm_gain, bias_table, inside)
    update, grad_tokens, grad_qkv, grad_out, grad_gain, grad_bias_sum = lax.map(crop_pass, (tokens, tile_ids, update_grad))
    grad_bias = jnp.einsum('hqk,oqk->ho', lax.optimization_barrier(jnp.sum(grad_bias_sum, axis=0)), onehot, precision=lax.Precision.HIGHEST)
    return (update, grad_tokens, lax.optimization_barrier(jnp.sum(grad_qkv, axis=0)), lax.optimization_barrier(jnp.sum(grad_out, axis=0)), lax.optimization_barrier(jnp.sum(grad_gain, axis=0)), grad_bias)
```

```python
import functools

import jax
import jax.numpy as jnp
from jax import lax
from jax.experimental import pallas as pl
from jax.experimental.pallas import tpu as pltpu
from jax.sharding import PartitionSpec as P

D = 512
HEADS = 8
HD = 32
INNER = 256
TILE = 8
HALO = 3
REG = 4
CAP = 2
ROWS = 128
CELLS = TILE * TILE
DP = 32
NX = 4
NY = 8
REGIONS = 9
OWN = 4
TILES = REGIONS * CAP
BROWS = HEADS * CELLS
CHUNK = 128
CHUNKS = BROWS // CHUNK
FAR = 9
SCALE = HD ** (-0.5)
WROWS = 64
SMALL = 16
CORES = [[0, 1], [2, 3]]
XS = [[x * NY + y for x in range(NX)] for y in range(NY)]
YS = [[x * NY + y for y in range(NY)] for x in range(NX)]
F32 = jnp.float32
BF = jnp.bfloat16
NT = (((1,), (1,)), ((), ()))
TN = (((0,), (0,)), ((), ()))
VM = pl.BlockSpec(memory_space=pltpu.VMEM)
SM = pl.BlockSpec(memory_space=pltpu.SMEM)


def dot(a, b, dims=(((1,), (0,)), ((), ()))):
    return lax.dot_general(a, b, dims, preferred_element_type=F32)


def call(body, outs, ins, scratch=(), limit=16, flops=1000000, traffic=1000000):
    single = not isinstance(outs, (list, tuple))
    return pl.pallas_call(
        body,
        out_shape=outs,
        in_specs=ins,
        out_specs=VM if single else [VM] * len(outs),
        scratch_shapes=list(scratch),
        compiler_params=pltpu.CompilerParams(vmem_limit_bytes=limit * 2**20),
        cost_estimate=pl.CostEstimate(flops=flops, bytes_accessed=traffic, transcendentals=0),
    )


def shape(dims, dtype):
    return jax.ShapeDtypeStruct(dims, dtype)


def pack_body(place, wq, wo, tok, grad, w_out, x_out):
    core = place[2]

    def half(c):
        rows = [wq[:, (3 * c + j) * 128 : (3 * c + j + 1) * 128].astype(F32) for j in range(3)]
        rows += [wo[:, (2 * c + j) * 128 : (2 * c + j + 1) * 128].astype(F32) for j in range(2)]
        block = jnp.concatenate(rows, axis=0).astype(BF)
        for d in range(DP):
            w_out[d] = block

    pl.when(core == 0)(lambda: half(0))
    pl.when(core == 1)(lambda: half(1))
    x_out[:, 0:D] = tok[...]
    x_out[:, D : 2 * D] = grad[...]


def table_body(base_ref, tab):
    query = lax.broadcasted_iota(jnp.int32, (CELLS, 128), 0)
    lane = lax.broadcasted_iota(jnp.int32, (CELLS, 128), 1)
    key = lane & 63
    left = lane < 64
    row_step = (key >> 3) - (query >> 3)
    col_step = (key & 7) - (query & 7)
    base = base_ref[...]
    for place in range(9):
        down, across = place // 3 - 1, place % 3 - 1
        shift = 64 * down + 8 * across
        inside = (jnp.abs(row_step + 8 * down) <= HALO) & (jnp.abs(col_step + 8 * across) <= HALO)
        first = pltpu.roll(base, (-shift - 27) % 128, 1)
        second = pltpu.roll(base, (64 - shift - 27) % 128, 1)
        for h in range(HEADS):
            a = pltpu.roll(
                jnp.broadcast_to(first[h : h + 1], (CELLS, 128)), 0, 1, stride=1, stride_axis=0
            )
            b = pltpu.roll(
                jnp.broadcast_to(second[h : h + 1], (CELLS, 128)), 0, 1, stride=1, stride_axis=0
            )
            tab[place, h * CELLS : (h + 1) * CELLS, :] = jnp.where(
                inside, jnp.where(left, a, b), -jnp.inf
            )
    tab[FAR] = jnp.full((BROWS, 128), -jnp.inf, F32)


def main_body(
    place,
    tiles,
    left,
    mid,
    right,
    w_mine,
    w_other,
    gain,
    tab,
    update,
    grad_tokens,
    sums,
    crow,
    ccol,
    blocks,
    wq,
    wo,
    normed,
    qkv,
    gatt,
    qbd,
    gbd,
    scores,
    dprobs,
    top,
    total,
    delta,
    pbf,
    dsf,
    att,
    dq,
    attended,
    dqkv,
    dk,
    dv,
    hist,
    rowsum,
):
    my_row, my_col, core = place[0], place[1], place[2]

    def assemble(pair):
        for c, w in enumerate(pair):
            for j in range(3):
                wq[:, (3 * c + j) * 128 : (3 * c + j + 1) * 128] = w[
                    :, 16 * j : 16 * j + 16, :
                ].reshape(D, 128)
            both = w[:, 48:64, :].astype(F32)
            for j in range(2):
                wo[:, (2 * c + j) * 128 : (2 * c + j + 1) * 128] = (
                    both[:, 8 * j : 8 * j + 8, :].reshape(INNER, 128).astype(BF)
                )

    pl.when(core == 0)(lambda: assemble((w_mine, w_other)))
    pl.when(core == 1)(lambda: assemble((w_other, w_mine)))

    for t in range(TILES):
        r = t // CAP
        ry, rx = my_row + r // 3 - 1, my_col + r % 3 - 1
        there = (ry >= 0) & (ry < 4) & (rx >= 0) & (rx < 4)
        tile = tiles[jnp.clip(ry, 0, 3), jnp.clip(rx, 0, 3), t % CAP]
        crow[t] = jnp.where(there, ry * REG + (tile >> 2), -1000 * (t + 1))
        ccol[t] = jnp.where(there, rx * REG + (tile & 3), -1000 * (t + 1))

    gain_row = gain[...]
    for r in range(REGIONS):
        source = (left, mid, right)[r % 3]
        x = source[r // 3, :, 0:D].astype(F32)
        inv = lax.rsqrt(jnp.mean(x * x, axis=-1, keepdims=True) + 1e-06)
        n = (x * inv * gain_row).astype(BF)
        normed[r * ROWS : (r + 1) * ROWS, :] = n
        qkv[r * ROWS : (r + 1) * ROWS, :] = dot(n, wq[...]).astype(BF)
        gatt[r * ROWS : (r + 1) * ROWS, :] = dot(
            source[r // 3, :, D : 2 * D], wo[...], NT
        ).astype(BF)

    dk[...] = jnp.zeros_like(dk)
    dv[...] = jnp.zeros_like(dv)
    hist[...] = jnp.zeros_like(hist)
    head_of = lax.broadcasted_iota(jnp.int32, (1, INNER), 1) >> 5
    masks = [(head_of == h).astype(F32) for h in range(HEADS)]
    masks_bf = [m.astype(BF) for m in masks]
    lane = lax.broadcasted_iota(jnp.int32, (CHUNK, 128), 1)
    first_slot = lane < 64
    flip = ((lane ^ lax.broadcasted_iota(jnp.int32, (CHUNK, 128), 0)) == 63).astype(F32).astype(BF)

    def near(a, b):
        return (jnp.abs(crow[a] - crow[b]) <= 1) & (jnp.abs(ccol[a] - ccol[b]) <= 1)

    def offset(a, b):
        index = (crow[b] - crow[a] + 1) * 3 + ccol[b] - ccol[a] + 1
        return jnp.where(near(a, b), index, FAR)

    def process(i, own):
        at = pl.multiple_of(i * CELLS, CELLS)
        queries = qkv[pl.ds(at, CELLS), 0:INNER]
        grads = gatt[pl.ds(at, CELLS), :]
        for h in range(HEADS):
            qbd[h * CELLS : (h + 1) * CELLS, :] = queries * masks_bf[h]
            gbd[h * CELLS : (h + 1) * CELLS, :] = grads * masks_bf[h]
        count = jnp.int32(0)
        own_block = jnp.int32(0)
        for r in range(REGIONS):
            blocks[count] = r
            if r == OWN:
                own_block = count
            count = count + (near(i, 2 * r) | near(i, 2 * r + 1)).astype(jnp.int32)
        top[...] = jnp.full(top.shape, -jnp.inf, F32)
        total[...] = jnp.zeros_like(total)
        delta[...] = jnp.zeros_like(delta)

        def pass_a(b, carry):
            r = blocks[b]
            k_at = pl.multiple_of(r * ROWS, ROWS)
            keys = qkv[pl.ds(k_at, ROWS), INNER : 2 * INNER]
            values = qkv[pl.ds(k_at, ROWS), 2 * INNER : 3 * INNER]
            off_a, off_b = offset(i, 2 * r), offset(i, 2 * r + 1)
            for c in range(CHUNKS):
                rows = slice(c * CHUNK, (c + 1) * CHUNK)
                bias = jnp.where(first_slot, tab[off_a, rows, :], tab[off_b, rows, :])
                s = dot(qbd[rows, :], keys, NT) * SCALE + bias
                scores[b, rows, :] = s
                top[rows, :] = jnp.maximum(top[rows, :], s)
                dprobs[b, rows, :] = dot(gbd[rows, :], values, NT)
            return carry

        lax.fori_loop(0, count, pass_a, 0)
        for c in range(CHUNKS):
            rows = slice(c * CHUNK, (c + 1) * CHUNK)
            top[rows, :] = jnp.broadcast_to(
                jnp.max(top[rows, :], axis=-1, keepdims=True), (CHUNK, 128)
            )

        def pass_b(b, carry):
            for c in range(CHUNKS):
                rows = slice(c * CHUNK, (c + 1) * CHUNK)
                e = jnp.exp(scores[b, rows, :] - top[rows, :])
                scores[b, rows, :] = e
                total[rows, :] += e
                delta[rows, :] += e * dprobs[b, rows, :]
            return carry

        lax.fori_loop(0, count, pass_b, 0)
        for c in range(CHUNKS):
            rows = slice(c * CHUNK, (c + 1) * CHUNK)
            inverse = 1.0 / jnp.sum(total[rows, :], axis=-1, keepdims=True)
            d = jnp.sum(delta[rows, :], axis=-1, keepdims=True) * inverse
            total[rows, :] = jnp.broadcast_to(inverse, (CHUNK, 128))
            delta[rows, :] = jnp.broadcast_to(d, (CHUNK, 128))
        if own:
            att[...] = jnp.zeros_like(att)
            dq[...] = jnp.zeros_like(dq)

        def probs_of(b):
            for c in range(CHUNKS):
                rows = slice(c * CHUNK, (c + 1) * CHUNK)
                p = scores[b, rows, :] * total[rows, :]
                pbf[rows, :] = p.astype(BF)
                dsf[rows, :] = (p * (dprobs[b, rows, :] - delta[rows, :])).astype(BF)

        def to_keys():
            dk[...] += dot(dsf[...], qbd[...], TN)
            dv[...] += dot(pbf[...], gbd[...], TN)

        def pass_c(b, carry):
            r = blocks[b]
            k_at = pl.multiple_of(r * ROWS, ROWS)
            keys = qkv[pl.ds(k_at, ROWS), INNER : 2 * INNER]
            values = qkv[pl.ds(k_at, ROWS), 2 * INNER : 3 * INNER]
            probs_of(b)
            pl.when(r == OWN)(to_keys)
            att_sum = att[...]
            dq_sum = dq[...]
            for h in range(HEADS):
                rows = slice(h * CELLS, (h + 1) * CELLS)
                att_sum += dot(pbf[rows, :], values) * masks[h]
                dq_sum += dot(dsf[rows, :], keys) * masks[h]
            att[...] = att_sum
            dq[...] = dq_sum
            half = first_slot[0:CELLS]
            for c in range(CHUNKS):
                flipped = dot(flip, dsf[c * CHUNK : (c + 1) * CHUNK, :])
                for h in range(2):
                    ds = flipped[h * CELLS : (h + 1) * CELLS, :]
                    for s, part in enumerate((jnp.where(half, ds, 0.0), jnp.where(half, 0.0, ds))):
                        turned = pltpu.roll(part, 0, 1, stride=1, stride_axis=0)
                        rowsum[s, 2 * c + h : 2 * c + h + 1, :] = jnp.sum(
                            turned, axis=0, keepdims=True
                        )
            for s in range(CAP):
                t = 2 * r + s
                shift = 64 * (crow[t] - crow[i]) + 8 * (ccol[t] - ccol[i]) - 36 - 64 * s
                shift = jnp.where(near(i, t), shift, 0) + 256
                hist[...] += pltpu.roll(rowsum[s], shift & 127, 1)
            return carry

        if own:
            lax.fori_loop(0, count, pass_c, 0)
            slot_at = pl.multiple_of((i - OWN * CAP) * CELLS, CELLS)
            attended[pl.ds(slot_at, CELLS), :] = att[...].astype(BF)
            dqkv[pl.ds(slot_at, CELLS), 0:INNER] = (dq[...] * SCALE).astype(BF)
        else:
            probs_of(own_block)
            to_keys()

    def own_step(s, carry):
        process(OWN * CAP + s, True)
        return carry

    lax.fori_loop(0, CAP, own_step, 0)

    def other_step(i, carry):
        t = i + jnp.where(i >= OWN * CAP, CAP, 0)
        pl.when(near(t, OWN * CAP) | near(t, OWN * CAP + 1))(lambda: process(t, False))
        return carry

    lax.fori_loop(0, TILES - CAP, other_step, 0)

    dqkv[:, INNER : 2 * INNER] = (dk[...] * SCALE).astype(BF)
    dqkv[:, 2 * INNER : 3 * INNER] = dv[...].astype(BF)
    update[...] = dot(attended[...], wo[...]).astype(BF)
    grad_out = dot(attended[...], mid[1, :, D : 2 * D], TN)
    for c in range(2):
        pair = [
            grad_out[:, (2 * c + j) * 128 : (2 * c + j + 1) * 128].reshape(DP, 8, 128)
            for j in range(2)
        ]
        both = jnp.concatenate(pair, axis=1).astype(BF)
        for d in range(DP):
            sums[c, d * WROWS + 48 : d * WROWS + 64, :] = both[d]
    own_rows = slice(OWN * ROWS, (OWN + 1) * ROWS)
    for j in range(6):
        block = dot(normed[own_rows, :], dqkv[:, j * 128 : (j + 1) * 128], TN).astype(BF)
        for d in range(DP):
            at = d * WROWS + (j % 3) * 16
            sums[j // 3, at : at + 16, :] = block[d * 16 : (d + 1) * 16]
    d_normed = dot(dqkv[...], wq[...], NT)
    x = mid[1, :, 0:D].astype(F32)
    inv = lax.rsqrt(jnp.mean(x * x, axis=-1, keepdims=True) + 1e-06)
    scaled = d_normed * gain_row
    gain_sum = jnp.sum(d_normed * x * inv, axis=0, keepdims=True)
    grad_tokens[...] = (
        inv * scaled - x * (inv * inv * inv) * jnp.mean(scaled * x, axis=-1, keepdims=True)
    ).astype(BF)
    folded = hist[0:4, :] + pltpu.roll(hist[4:8, :], 64, 1)
    small = jnp.concatenate([gain_sum[:, j * 128 : (j + 1) * 128] for j in range(4)] + [folded], 0)
    split = halves(small)
    sums[0, DP * WROWS : DP * WROWS + SMALL, :] = split
    sums[1, DP * WROWS : DP * WROWS + SMALL, :] = split


def halves(value):
    high = value.astype(BF).astype(F32)
    return jnp.concatenate([high, value - high], axis=0).astype(BF)


def whole(value):
    wide = value.astype(F32)
    return wide[..., 0:8, :] + wide[..., 8:16, :]


def sum_body(senders, parts, span, received, out):
    rows = parts * span
    for p in range(parts):
        acc = received[0, p * span : (p + 1) * span, :].astype(F32)
        for s in range(1, senders):
            acc += received[s, p * span : (p + 1) * span, :].astype(F32)
        out[p, 0:span, :] = acc.astype(BF)
    small = whole(received[0, rows : rows + SMALL, :])
    for s in range(1, senders):
        small += whole(received[s, rows : rows + SMALL, :])
    split = halves(small)
    for p in range(parts):
        out[p, span : span + SMALL, :] = split


def last_sum_body(received, out):
    acc = received[0, 0:WROWS, :].astype(F32)
    small = whole(received[0, WROWS : WROWS + SMALL, :])
    for s in range(1, NY):
        acc += received[s, 0:WROWS, :].astype(F32)
        small += whole(received[s, WROWS : WROWS + SMALL, :])
    acc = acc.astype(BF)
    split = halves(small)
    for p in range(16):
        out[p, 0:WROWS, :] = acc
        out[p, WROWS : WROWS + SMALL, :] = split


def finish_body(received, grad_qkv, grad_out, grad_gain, grad_bias):
    small = None
    for c in range(2):
        acc = None
        for y in range(c, 4, 2):
            for x in range(4):
                part = received[4 * y + x, 0:WROWS, :].astype(F32)
                acc = part if acc is None else acc + part
                if c == 0:
                    more = whole(received[4 * y + x, WROWS : WROWS + SMALL, :])
                    small = more if small is None else small + more
        for j in range(3):
            grad_qkv[:, (3 * c + j) * 128 : (3 * c + j + 1) * 128] = acc[16 * j : 16 * j + 16, :]
        for j in range(2):
            at = 48 + 8 * j
            grad_out[:, (2 * c + j) * 128 : (2 * c + j + 1) * 128] = acc[at : at + 8, :]
    for j in range(4):
        grad_gain[:, j * 128 : (j + 1) * 128] = small[j : j + 1, :]
    folded = small[4:8, :]
    table = jnp.concatenate([folded, pltpu.roll(folded, 64, 1)], axis=0)
    lane = lax.broadcasted_iota(jnp.int32, (HEADS, 128), 1)
    out = jnp.zeros((HEADS, 128), F32)
    for r in range(7):
        moved = table if r == 0 else pltpu.roll(table, 128 - r, 1)
        out = jnp.where((lane >= 7 * r) & (lane < 7 * r + 7), moved, out)
    grad_bias[...] = out[:, 0:49]


def shards(tokens, tile_ids, w_qkv, w_out, norm_gain, rel_bias, update_grad):
    my_row = lax.axis_index("gy")
    my_col = lax.axis_index("gx")
    place = jnp.stack([my_row, my_col, my_row % 2]).astype(jnp.int32)
    swap = [(0, 1), (1, 0), (2, 3), (3, 2)]
    forth = [(0, 1), (1, 2), (2, 3)]
    back = [(1, 0), (2, 1), (3, 2)]

    w_send, rows = call(
        pack_body,
        [shape((DP, WROWS, 128), BF), shape((ROWS, 2 * D), BF)],
        [SM, VM, VM, VM, VM],
    )(place, w_qkv, w_out, tokens.reshape(ROWS, D), update_grad.reshape(ROWS, D))
    above = lax.ppermute(rows, "gy", forth)
    below = lax.ppermute(rows, "gy", back)
    w_mine = lax.all_to_all(w_send, "dp", 0, 0, tiled=True)
    mid = jnp.stack([above, rows, below])
    left = lax.ppermute(mid, "gx", forth)
    right = lax.ppermute(mid, "gx", back)
    w_other = lax.ppermute(w_mine, "gy", swap)

    base = jnp.pad(rel_bias.reshape(HEADS, 7, 7), ((0, 0), (0, 0), (0, 1))).reshape(HEADS, 56)
    base = jnp.pad(base, ((0, 0), (0, 72)))
    table = call(table_body, shape((10, BROWS, 128), F32), [VM])(base)

    f32 = lambda *dims: pltpu.VMEM(dims, F32)
    bf = lambda *dims: pltpu.VMEM(dims, BF)
    update, grad_tokens, sums = call(
        main_body,
        [
            shape((ROWS, D), BF),
            shape((ROWS, D), BF),
            shape((2, DP * WROWS + SMALL, 128), BF),
        ],
        [SM, SM] + [VM] * 7,
        [
            pltpu.SMEM((TILES,), jnp.int32),
            pltpu.SMEM((TILES,), jnp.int32),
            pltpu.SMEM((REGIONS + 1,), jnp.int32),
            bf(D, 3 * INNER),
            bf(INNER, D),
            bf(REGIONS * ROWS, D),
            bf(REGIONS * ROWS, 3 * INNER),
            bf(REGIONS * ROWS, INNER),
            bf(BROWS, INNER),
            bf(BROWS, INNER),
            f32(4, BROWS, 128),
            f32(4, BROWS, 128),
            f32(BROWS, 128),
            f32(BROWS, 128),
            f32(BROWS, 128),
            bf(BROWS, 128),
            bf(BROWS, 128),
            f32(CELLS, INNER),
            f32(CELLS, INNER),
            bf(ROWS, INNER),
            bf(ROWS, 3 * INNER),
            f32(ROWS, INNER),
            f32(ROWS, INNER),
            f32(HEADS, 128),
            f32(CAP, HEADS, 128),
        ],
        limit=40,
        flops=4000000000,
        traffic=12000000,
    )(
        place,
        tile_ids.reshape(4, 4, CAP),
        left,
        mid,
        right,
        w_mine,
        w_other,
        norm_gain.reshape(1, D),
        table,
    )

    got = lax.all_to_all(sums, "gy", 0, 0, tiled=True, axis_index_groups=CORES)
    got = call(
        functools.partial(sum_body, 2, NX, NY * WROWS),
        shape((NX, NY * WROWS + SMALL, 128), BF),
        [VM],
    )(got)
    got = lax.all_to_all(got, "dp", 0, 0, tiled=True, axis_index_groups=XS)
    got = call(
        functools.partial(sum_body, NX, NY, WROWS), shape((NY, WROWS + SMALL, 128), BF), [VM]
    )(got)
    got = lax.all_to_all(got, "dp", 0, 0, tiled=True, axis_index_groups=YS)
    got = call(last_sum_body, shape((16, WROWS + SMALL, 128), BF), [VM])(got)
    got = lax.all_to_all(got, ("gy", "gx"), 0, 0, tiled=True)
    grad_qkv, grad_out, grad_gain, grad_bias = call(
        finish_body,
        [
            shape((16, 3 * INNER), F32),
            shape((8, D), F32),
            shape((1, D), F32),
            shape((HEADS, 49), F32),
        ],
        [VM],
    )(got)
    return (
        update.reshape(tokens.shape),
        grad_tokens.reshape(tokens.shape),
        grad_qkv,
        grad_out,
        grad_gain.reshape(D),
        grad_bias,
    )


def solution(mesh):
    return jax.shard_map(
        shards,
        mesh=mesh,
        in_specs=(
            P("dp", "gy", "gx", None, None),
            P("dp", None, None, None),
            P("dp", None),
            P("dp", None),
            P(),
            P(),
            P("dp", "gy", "gx", None, None),
        ),
        out_specs=(
            P("dp", "gy", "gx", None, None),
            P("dp", "gy", "gx", None, None),
            P("dp", None),
            P("dp", None),
            P(),
            P(),
        ),
        check_vma=False,
    )
```

```python
import functools

import jax
import jax.numpy as jnp
from jax import lax
from jax.experimental import pallas as pl
from jax.experimental.pallas import tpu as pltpu
from jax.sharding import PartitionSpec as P

D = 512
HEADS = 8
HD = 32
INNER = 256
TILE = 8
HALO = 3
REG = 4
CAP = 2
ROWS = 128
CELLS = TILE * TILE
DP = 32
NX = 4
NY = 8
PAIRS = 7
TILES = PAIRS * 2
BROWS = HEADS * CELLS
T_ROWS = 48
G_ROWS = 32
STRIP = T_ROWS + G_ROWS
MESSAGE = 2 * ROWS + 2 * STRIP
CHUNK = 128
FAR = 9
SCALE = HD ** (-0.5)
WROWS = 64
SMALL = 16
CORES = [[0, 1], [2, 3]]
XS = [[x * NY + y for x in range(NX)] for y in range(NY)]
YS = [[x * NY + y for y in range(NY)] for x in range(NX)]
ZS = [[0, 1, 2, 3, 8, 9, 10, 11], [4, 5, 6, 7, 12, 13, 14, 15]]
F32 = jnp.float32
BF = jnp.bfloat16
NT = (((1,), (1,)), ((), ()))
TN = (((0,), (0,)), ((), ()))
VM = pl.BlockSpec(memory_space=pltpu.VMEM)
SM = pl.BlockSpec(memory_space=pltpu.SMEM)
HBM = pl.BlockSpec(memory_space=pltpu.HBM)


def dot(a, b, dims=(((1,), (0,)), ((), ()))):
    return lax.dot_general(a, b, dims, preferred_element_type=F32)


def call(body, outs, ins, scratch=(), limit=16, flops=1000000, traffic=1000000):
    single = not isinstance(outs, (list, tuple))
    return pl.pallas_call(
        body,
        out_shape=outs,
        in_specs=ins,
        out_specs=VM if single else [VM] * len(outs),
        scratch_shapes=list(scratch),
        compiler_params=pltpu.CompilerParams(vmem_limit_bytes=limit * 2**20),
        cost_estimate=pl.CostEstimate(flops=flops, bytes_accessed=traffic, transcendentals=0),
    )


def shape(dims, dtype):
    return jax.ShapeDtypeStruct(dims, dtype)


def pack_body(wq_in, wo_in, tok_in, grad_in, w_out, rows, down, up, wq, wo, sems):
    copies = [
        pltpu.make_async_copy(wq_in, wq, sems.at[0]),
        pltpu.make_async_copy(wo_in, wo, sems.at[1]),
        pltpu.make_async_copy(tok_in, rows.at[pl.ds(0, ROWS)], sems.at[2]),
        pltpu.make_async_copy(grad_in, rows.at[pl.ds(ROWS, ROWS)], sems.at[3]),
    ]
    for copy in copies:
        copy.start()
    copies[0].wait()
    copies[1].wait()
    parts = []
    for c in range(2):
        parts += [wq[:, (3 * c + j) * 128 : (3 * c + j + 1) * 128].astype(F32) for j in range(3)]
        parts += [wo[:, (2 * c + j) * 128 : (2 * c + j + 1) * 128].astype(F32) for j in range(2)]
    block = jnp.concatenate(parts, axis=0).astype(BF)
    for d in range(DP):
        w_out[d] = block
    copies[2].wait()
    copies[3].wait()
    for s in range(CAP):
        t, g = s * CELLS, ROWS + s * CELLS
        down[s, 0:T_ROWS, :] = rows[t + CELLS - T_ROWS : t + CELLS, :]
        down[s, T_ROWS:STRIP, :] = rows[g + CELLS - G_ROWS : g + CELLS, :]
        up[s, 0:T_ROWS, :] = rows[t : t + T_ROWS, :]
        up[s, T_ROWS:STRIP, :] = rows[g : g + G_ROWS, :]


def corner_body(place, tiles, rows, above, below, to_right, to_left):
    over = jnp.maximum(place[0] - 1, 0)
    under = jnp.minimum(place[0] + 1, 3)
    col = place[1]
    for out, top, bottom in ((to_right, 15, 3), (to_left, 12, 0)):
        out[0 : 2 * ROWS, :] = rows[...]
        out[2 * ROWS : 2 * ROWS + STRIP, :] = above[
            (tiles[over, col, 1] == top).astype(jnp.int32)
        ]
        out[2 * ROWS + STRIP : MESSAGE, :] = below[
            (tiles[under, col, 1] == bottom).astype(jnp.int32)
        ]


def plan_tiles(place, tiles, plan, crow, ccol):
    my_row, my_col = place[0], place[1]
    steps = [(0, 0)] * 2 + [(-1, 0)] * 2 + [(1, 0)] * 2 + [(0, -1)] * 2 + [(0, 1)] * 2
    corners = [(-1, -1, 15), (-1, 1, 12), (1, -1, 3), (1, 1, 0)]
    for t, (dy, dx, *corner) in enumerate(steps + corners):
        ry, rx = my_row + dy, my_col + dx
        there = (ry >= 0) & (ry < 4) & (rx >= 0) & (rx < 4)
        ty, tx = jnp.clip(ry, 0, 3), jnp.clip(rx, 0, 3)
        if corner:
            tile = jnp.int32(corner[0])
            there = there & ((tiles[ty, tx, 0] == tile) | (tiles[ty, tx, 1] == tile))
        else:
            tile = tiles[ty, tx, t % 2]
        crow[t] = jnp.where(there, ry * REG + (tile >> 2), -1000 * (t + 1))
        ccol[t] = jnp.where(there, rx * REG + (tile & 3), -1000 * (t + 1))

    def near(a, b):
        return (jnp.abs(crow[a] - crow[b]) <= 1) & (jnp.abs(ccol[a] - ccol[b]) <= 1)

    def tile_plan(t, carry):
        plan[t, 0] = (near(t, 0) | near(t, 1)).astype(jnp.int32)
        count = jnp.int32(0)
        for r in range(PAIRS):
            plan[t, 2 + count] = r
            both = jnp.int32(0)
            for s in range(2):
                k = 2 * r + s
                close = near(t, k)
                down, across = crow[k] - crow[t], ccol[k] - ccol[t]
                plan[t, 10 + 8 * s + count] = jnp.where(close, down * 3 + across + 4, FAR)
                plan[t, 26 + 8 * s + count] = jnp.where(
                    close, (64 * down + 8 * across + 512) & 127, 0
                )
                both = both | close.astype(jnp.int32)
            count = count + both
        plan[t, 1] = count
        return carry

    lax.fori_loop(0, TILES, tile_plan, 0)


def table_body(place, tiles, base_ref, tab, plan, crow, ccol):
    plan_tiles(place, tiles, plan, crow, ccol)
    query = lax.broadcasted_iota(jnp.int32, (CELLS, 128), 0)
    lane = lax.broadcasted_iota(jnp.int32, (CELLS, 128), 1)
    key = lane & 63
    left = lane < 64
    row_step = (key >> 3) - (query >> 3)
    col_step = (key & 7) - (query & 7)
    base = base_ref[...]
    for place in range(9):
        down, across = place // 3 - 1, place % 3 - 1
        shift = 64 * down + 8 * across
        inside = (jnp.abs(row_step + 8 * down) <= HALO) & (jnp.abs(col_step + 8 * across) <= HALO)
        first = pltpu.roll(base, (-shift - 27) % 128, 1)
        second = pltpu.roll(base, (64 - shift - 27) % 128, 1)
        for h in range(HEADS):
            a = pltpu.roll(
                jnp.broadcast_to(first[h : h + 1], (CELLS, 128)), 0, 1, stride=1, stride_axis=0
            )
            b = pltpu.roll(
                jnp.broadcast_to(second[h : h + 1], (CELLS, 128)), 0, 1, stride=1, stride_axis=0
            )
            tab[place, h * CELLS : (h + 1) * CELLS, :] = jnp.where(
                inside, jnp.where(left, a, b), -jnp.inf
            )
    tab[FAR] = jnp.full((BROWS, 128), -jnp.inf, F32)


def prep_body(rows, above, below, left, right, gain, out):
    normed = out.at[pl.ds(0, PAIRS * ROWS)]
    grads = out.at[pl.ds(PAIRS * ROWS, PAIRS * ROWS)]
    own = out.at[pl.ds(2 * PAIRS * ROWS, ROWS)]
    gain_row = gain[...]

    def norm(block):
        x = block.astype(F32)
        inv = lax.rsqrt(jnp.mean(x * x, axis=-1, keepdims=True) + 1e-06)
        return (x * inv * gain_row).astype(BF)

    own[...] = rows[0:ROWS, :]
    for t, source in ((0, rows), (6, left), (8, right)):
        at = t * CELLS
        normed[at : at + ROWS, :] = norm(source[0:ROWS, :])
        grads[at : at + ROWS, :] = source[ROWS : 2 * ROWS, :]
    at_a, at_b = 2 * ROWS, 2 * ROWS + STRIP
    upper = [
        (2, above[0]),
        (3, above[1]),
        (10, left[at_a : at_a + STRIP, :]),
        (11, right[at_a : at_a + STRIP, :]),
    ]
    lower = [
        (4, below[0]),
        (5, below[1]),
        (12, left[at_b : at_b + STRIP, :]),
        (13, right[at_b : at_b + STRIP, :]),
    ]
    for t, strip in upper:
        at = t * CELLS
        normed[at : at + CELLS - T_ROWS, :] = jnp.zeros((CELLS - T_ROWS, D), BF)
        normed[at + CELLS - T_ROWS : at + CELLS, :] = norm(strip[0:T_ROWS])
        grads[at : at + CELLS - G_ROWS, :] = jnp.zeros((CELLS - G_ROWS, D), BF)
        grads[at + CELLS - G_ROWS : at + CELLS, :] = strip[T_ROWS:STRIP]
    for t, strip in lower:
        at = t * CELLS
        normed[at : at + T_ROWS, :] = norm(strip[0:T_ROWS])
        normed[at + T_ROWS : at + CELLS, :] = jnp.zeros((CELLS - T_ROWS, D), BF)
        grads[at : at + G_ROWS, :] = strip[T_ROWS:STRIP]
        grads[at + G_ROWS : at + CELLS, :] = jnp.zeros((CELLS - G_ROWS, D), BF)


def main_body(
    plan,
    packed,
    weights,
    gain,
    tab,
    update,
    grad_tokens,
    sums,
    wq,
    wo,
    qkv,
    gatt,
    qbd,
    gbd,
    scores,
    dprobs,
    top,
    total,
    delta,
    pbf,
    dsf,
    att,
    dq,
    attended,
    dqkv,
    dk,
    dv,
    hist,
    rowsum,
):
    normed = packed.at[pl.ds(0, PAIRS * ROWS)]
    grads = packed.at[pl.ds(PAIRS * ROWS, PAIRS * ROWS)]
    tokens = packed.at[pl.ds(2 * PAIRS * ROWS, ROWS)]
    for c in range(2):
        for j in range(3):
            at = WROWS * c + 16 * j
            wq[:, (3 * c + j) * 128 : (3 * c + j + 1) * 128] = weights[
                :, at : at + 16, :
            ].reshape(D, 128)
        both = weights[:, WROWS * c + 48 : WROWS * c + 64, :].astype(F32)
        for j in range(2):
            wo[:, (2 * c + j) * 128 : (2 * c + j + 1) * 128] = (
                both[:, 8 * j : 8 * j + 8, :].reshape(INNER, 128).astype(BF)
            )

    gain_row = gain[...]
    for j in range(3):
        cols = slice(j * INNER, (j + 1) * INNER)
        qkv[:, cols] = dot(normed[...], wq[:, cols]).astype(BF)
    gatt[...] = dot(grads[...], wo[...], NT).astype(BF)

    dk[...] = jnp.zeros_like(dk)
    dv[...] = jnp.zeros_like(dv)
    hist[...] = jnp.zeros_like(hist)
    head_of = lax.broadcasted_iota(jnp.int32, (1, INNER), 1) >> 5
    masks_bf = [(head_of == h).astype(F32).astype(BF) for h in range(HEADS)]
    lane = lax.broadcasted_iota(jnp.int32, (CHUNK, 128), 1)
    first_slot = lane < 64
    lane_masks = [((lane[0:CELLS] >> 5) == h).astype(F32) for h in range(4)]
    mirror = ((lane + lax.broadcasted_iota(jnp.int32, (128, 128), 0)) == 127).astype(F32)
    mirror_bf = mirror.astype(BF)

    def process(i, own, q_at, nq):
        per = CHUNK // nq
        chunks = HEADS // per
        used = HEADS * nq
        at = pl.multiple_of(i * CELLS, CELLS) + q_at
        queries = qkv[pl.ds(at, nq), 0:INNER]
        cotangents = gatt[pl.ds(at, nq), :]
        for h in range(HEADS):
            qbd[h * nq : (h + 1) * nq, :] = queries * masks_bf[h]
            gbd[h * nq : (h + 1) * nq, :] = cotangents * masks_bf[h]
        count = plan[i, 1]

        def bias_of(off, c):
            parts = [
                tab[off, (c * per + h) * CELLS + q_at : (c * per + h) * CELLS + q_at + nq, :]
                for h in range(per)
            ]
            return jnp.concatenate(parts, axis=0)

        def pass_a(b, first):
            k_at = pl.multiple_of(plan[i, 2 + b] * ROWS, ROWS)
            keys = qkv[pl.ds(k_at, ROWS), INNER : 2 * INNER]
            values = qkv[pl.ds(k_at, ROWS), 2 * INNER : 3 * INNER]
            off_a, off_b = plan[i, 10 + b], plan[i, 18 + b]
            scores[b, 0:used, :] = dot(qbd[0:used, :], keys, NT)
            dprobs[b, 0:used, :] = dot(gbd[0:used, :], values, NT)
            for c in range(chunks):
                rows = slice(c * CHUNK, (c + 1) * CHUNK)
                bias = jnp.where(first_slot, bias_of(off_a, c), bias_of(off_b, c))
                s = scores[b, rows, :] * SCALE + bias
                scores[b, rows, :] = s
                top[rows, :] = s if first else jnp.maximum(top[rows, :], s)

        def rest_a(b, carry):
            pass_a(b, False)
            return carry

        pass_a(0, True)
        lax.fori_loop(1, count, rest_a, 0)
        for c in range(chunks):
            rows = slice(c * CHUNK, (c + 1) * CHUNK)
            top[rows, :] = jnp.broadcast_to(
                jnp.max(top[rows, :], axis=-1, keepdims=True), (CHUNK, 128)
            )

        def pass_b(b, first):
            for c in range(chunks):
                rows = slice(c * CHUNK, (c + 1) * CHUNK)
                e = jnp.exp(scores[b, rows, :] - top[rows, :])
                d = e * dprobs[b, rows, :]
                scores[b, rows, :] = e
                total[rows, :] = e if first else total[rows, :] + e
                delta[rows, :] = d if first else delta[rows, :] + d

        def rest_b(b, carry):
            pass_b(b, False)
            return carry

        pass_b(0, True)
        lax.fori_loop(1, count, rest_b, 0)
        for c in range(chunks):
            rows = slice(c * CHUNK, (c + 1) * CHUNK)
            inverse = 1.0 / jnp.sum(total[rows, :], axis=-1, keepdims=True)
            d = jnp.sum(delta[rows, :], axis=-1, keepdims=True) * inverse
            total[rows, :] = jnp.broadcast_to(inverse, (CHUNK, 128))
            delta[rows, :] = jnp.broadcast_to(d, (CHUNK, 128))

        def probs_of(b):
            for c in range(chunks):
                rows = slice(c * CHUNK, (c + 1) * CHUNK)
                p = scores[b, rows, :] * total[rows, :]
                pbf[rows, :] = p.astype(BF)
                dsf[rows, :] = (p * (dprobs[b, rows, :] - delta[rows, :])).astype(BF)

        def pass_c(b, first):
            k_at = pl.multiple_of(plan[i, 2 + b] * ROWS, ROWS)
            keys = qkv[pl.ds(k_at, ROWS), INNER : 2 * INNER]
            values = qkv[pl.ds(k_at, ROWS), 2 * INNER : 3 * INNER]
            probs_of(b)
            for sum_ref, factor, other in ((att, pbf, values), (dq, dsf, keys)):
                wide = dot(factor[...], other)
                for n in range(2):
                    cols = slice(n * 128, (n + 1) * 128)
                    acc = None if first else sum_ref[:, cols]
                    for h in range(4 * n, 4 * n + 4):
                        part = wide[h * CELLS : (h + 1) * CELLS, cols] * lane_masks[h & 3]
                        acc = part if acc is None else acc + part
                    sum_ref[:, cols] = acc
            flipped = dot(dsf[...], mirror_bf)
            half = first_slot[0:CELLS]
            for h in range(HEADS):
                ds = flipped[h * CELLS : (h + 1) * CELLS]
                for s, part in enumerate((jnp.where(half, 0.0, ds), jnp.where(half, ds, 0.0))):
                    turned = pltpu.roll(part, 0, 1, stride=1, stride_axis=0)
                    rowsum[s, h : h + 1, :] = jnp.sum(turned, axis=0, keepdims=True)
            for s in range(2):
                shift = (64 * s - 27 - plan[i, 26 + 8 * s + b] + 256) & 127
                hist[...] += pltpu.roll(rowsum[s], shift, 1)

        def rest_c(b, carry):
            pass_c(b, False)
            return carry

        if own:
            pass_c(0, True)
        else:
            probs_of(0)
        dk[...] += dot(dsf[0:used, :], qbd[0:used, :], TN)
        dv[...] += dot(pbf[0:used, :], gbd[0:used, :], TN)
        if own:
            lax.fori_loop(1, count, rest_c, 0)
            slot_at = pl.multiple_of(i * CELLS, CELLS)
            attended[pl.ds(slot_at, CELLS), :] = att[...].astype(BF)
            dqkv[pl.ds(slot_at, CELLS), 0:INNER] = (dq[...] * SCALE).astype(BF)

    def own_step(s, carry):
        process(s, True, 0, CELLS)
        return carry

    lax.fori_loop(0, 2, own_step, 0)

    def others(tile_of, q_at, nq):
        def step(n, carry):
            t = tile_of(n)
            pl.when(plan[t, 0] > 0)(lambda: process(t, False, q_at, nq))
            return carry

        lax.fori_loop(0, 4, step, 0)

    others(lambda n: n + 6, 0, CELLS)
    others(lambda n: n + jnp.where(n < 2, 2, 8), CELLS - G_ROWS, G_ROWS)
    others(lambda n: n + jnp.where(n < 2, 4, 10), 0, G_ROWS)

    dqkv[:, INNER : 2 * INNER] = (dk[...] * SCALE).astype(BF)
    dqkv[:, 2 * INNER : 3 * INNER] = dv[...].astype(BF)
    update[...] = dot(attended[...], wo[...]).astype(BF)
    grad_out = dot(attended[...], grads[0:ROWS, :], TN)
    for c in range(2):
        pair = [
            grad_out[:, (2 * c + j) * 128 : (2 * c + j + 1) * 128].reshape(DP, 8, 128)
            for j in range(2)
        ]
        both = jnp.concatenate(pair, axis=1).astype(BF)
        for d in range(DP):
            sums[c, d * WROWS + 48 : d * WROWS + 64, :] = both[d]
    for n in range(3):
        pair = dot(normed[0:ROWS, :], dqkv[:, n * 256 : (n + 1) * 256], TN).astype(BF)
        for j in (2 * n, 2 * n + 1):
            block = pair[:, (j - 2 * n) * 128 : (j - 2 * n + 1) * 128]
            for d in range(DP):
                at = d * WROWS + (j % 3) * 16
                sums[j // 3, at : at + 16, :] = block[d * 16 : (d + 1) * 16]
    d_normed = dot(dqkv[...], wq[...], NT)
    x = tokens[...].astype(F32)
    inv = lax.rsqrt(jnp.mean(x * x, axis=-1, keepdims=True) + 1e-06)
    scaled = d_normed * gain_row
    gain_sum = jnp.sum(d_normed * x * inv, axis=0, keepdims=True)
    grad_tokens[...] = (
        inv * scaled - x * (inv * inv * inv) * jnp.mean(scaled * x, axis=-1, keepdims=True)
    ).astype(BF)
    offsets = lax.dot_general(
        hist[...],
        mirror,
        (((1,), (0,)), ((), ())),
        precision=lax.Precision.HIGHEST,
        preferred_element_type=F32,
    )
    folded = offsets[0:4, :] + pltpu.roll(offsets[4:8, :], 64, 1)
    small = jnp.concatenate([gain_sum[:, j * 128 : (j + 1) * 128] for j in range(4)] + [folded], 0)
    split = halves(small)
    sums[0, DP * WROWS : DP * WROWS + SMALL, :] = split
    sums[1, DP * WROWS : DP * WROWS + SMALL, :] = split


def halves(value):
    high = value.astype(BF).astype(F32)
    return jnp.concatenate([high, value - high], axis=0).astype(BF)


def whole(value):
    wide = value.astype(F32)
    return wide[..., 0:8, :] + wide[..., 8:16, :]


def sum_body(senders, parts, span, received, out):
    rows = parts * span
    for p in range(parts):
        acc = received[0, p * span : (p + 1) * span, :].astype(F32)
        for s in range(1, senders):
            acc += received[s, p * span : (p + 1) * span, :].astype(F32)
        out[p, 0:span, :] = acc.astype(BF)
    small = whole(received[0, rows : rows + SMALL, :])
    for s in range(1, senders):
        small += whole(received[s, rows : rows + SMALL, :])
    split = halves(small)
    for p in range(parts):
        out[p, span : span + SMALL, :] = split


def last_sum_body(received, out):
    acc = received[0, 0:WROWS, :].astype(F32)
    small = whole(received[0, WROWS : WROWS + SMALL, :])
    for s in range(1, NY):
        acc += received[s, 0:WROWS, :].astype(F32)
        small += whole(received[s, WROWS : WROWS + SMALL, :])
    acc = acc.astype(BF)
    split = halves(small)
    for p in range(8):
        out[p, 0:WROWS, :] = acc
        out[p, WROWS : WROWS + SMALL, :] = split


def z_body(received, mine, small):
    acc = received[0, 0:WROWS, :].astype(F32)
    more = whole(received[0, WROWS : WROWS + SMALL, :])
    for s in range(1, 8):
        acc += received[s, 0:WROWS, :].astype(F32)
        more += whole(received[s, WROWS : WROWS + SMALL, :])
    mine[...] = acc.astype(BF)
    small[...] = more


def finish_body(place, mine, theirs, small_in, grad_qkv, grad_out, grad_gain, grad_bias):
    small = small_in[...]
    odd = place[0] & 1

    def unpack(pair):
        for c, ref in enumerate(pair):
            acc = ref[...].astype(F32)
            for j in range(3):
                at = (3 * c + j) * 128
                grad_qkv[:, at : at + 128] = acc[16 * j : 16 * j + 16, :]
            for j in range(2):
                at = 48 + 8 * j
                grad_out[:, (2 * c + j) * 128 : (2 * c + j + 1) * 128] = acc[at : at + 8, :]

    pl.when(odd == 0)(lambda: unpack((mine, theirs)))
    pl.when(odd == 1)(lambda: unpack((theirs, mine)))
    for j in range(4):
        grad_gain[:, j * 128 : (j + 1) * 128] = small[j : j + 1, :]
    folded = small[4:8, :]
    table = jnp.concatenate([folded, pltpu.roll(folded, 64, 1)], axis=0)
    lane = lax.broadcasted_iota(jnp.int32, (HEADS, 128), 1)
    out = jnp.zeros((HEADS, 128), F32)
    for r in range(7):
        moved = table if r == 0 else pltpu.roll(table, 128 - r, 1)
        out = jnp.where((lane >= 7 * r) & (lane < 7 * r + 7), moved, out)
    grad_bias[...] = out[:, 0:49]


def layer(plan, packed, weights, gain, table):
    f32 = lambda *dims: pltpu.VMEM(dims, F32)
    bf = lambda *dims: pltpu.VMEM(dims, BF)
    return call(
        main_body,
        [
            shape((ROWS, D), BF),
            shape((ROWS, D), BF),
            shape((2, DP * WROWS + SMALL, 128), BF),
        ],
        [SM] + [VM] * 4,
        [
            bf(D, 3 * INNER),
            bf(INNER, D),
            bf(PAIRS * ROWS, 3 * INNER),
            bf(PAIRS * ROWS, INNER),
            bf(BROWS, INNER),
            bf(BROWS, INNER),
            f32(4, BROWS, 128),
            f32(4, BROWS, 128),
            f32(BROWS, 128),
            f32(BROWS, 128),
            f32(BROWS, 128),
            bf(BROWS, 128),
            bf(BROWS, 128),
            f32(CELLS, INNER),
            f32(CELLS, INNER),
            bf(ROWS, INNER),
            bf(ROWS, 3 * INNER),
            f32(ROWS, INNER),
            f32(ROWS, INNER),
            f32(HEADS, 128),
            f32(CAP, HEADS, 128),
        ],
        limit=40,
        flops=4000000000,
        traffic=12000000,
    )(plan, packed, weights, gain, table)


def shards(tokens, tile_ids, w_qkv, w_out, norm_gain, rel_bias, update_grad):
    my_row = lax.axis_index("gy")
    my_col = lax.axis_index("gx")
    place = jnp.stack([my_row, my_col]).astype(jnp.int32)
    forth = [(0, 1), (1, 2), (2, 3)]
    back = [(1, 0), (2, 1), (3, 2)]

    tiles = tile_ids.reshape(4, 4, CAP)
    strip = shape((CAP, STRIP, D), BF)
    w_send, rows, down, up = call(
        pack_body,
        [shape((DP, 2 * WROWS, 128), BF), shape((2 * ROWS, D), BF), strip, strip],
        [HBM, HBM, HBM, HBM],
        [
            pltpu.VMEM((16, 3 * INNER), BF),
            pltpu.VMEM((8, D), BF),
            pltpu.SemaphoreType.DMA((4,)),
        ],
        limit=60,
    )(w_qkv, w_out, tokens.reshape(ROWS, D), update_grad.reshape(ROWS, D))
    above = lax.ppermute(down, "gy", forth)
    below = lax.ppermute(up, "gy", back)
    weights = lax.all_to_all(w_send, "dp", 0, 0, tiled=True)
    message = shape((MESSAGE, D), BF)
    to_right, to_left = call(corner_body, [message, message], [SM, SM, VM, VM, VM], flops=16000000000)(
        place, tiles, rows, above, below
    )
    left = lax.ppermute(to_right, "gx", forth)
    right = lax.ppermute(to_left, "gx", back)
    base = jnp.pad(rel_bias.reshape(HEADS, 7, 7), ((0, 0), (0, 0), (0, 1))).reshape(HEADS, 56)
    base = jnp.pad(base, ((0, 0), (0, 72)))
    table, plan = pl.pallas_call(
        table_body,
        out_shape=[shape((10, BROWS, 128), F32), shape((TILES, 48), jnp.int32)],
        in_specs=[SM, SM, VM],
        out_specs=[VM, SM],
        scratch_shapes=[pltpu.SMEM((TILES,), jnp.int32), pltpu.SMEM((TILES,), jnp.int32)],
        compiler_params=pltpu.CompilerParams(vmem_limit_bytes=16 * 2**20),
        cost_estimate=pl.CostEstimate(flops=2000000, bytes_accessed=4000000, transcendentals=0),
    )(place, tiles, base)
    packed = call(prep_body, shape((2 * PAIRS * ROWS + ROWS, D), BF), [VM] * 6)(
        rows, above, below, left, right, norm_gain.reshape(1, D)
    )
    update, grad_tokens, sums = layer(plan, packed, weights, norm_gain.reshape(1, D), table)

    got = lax.all_to_all(sums, "gy", 0, 0, tiled=True, axis_index_groups=CORES)
    got = call(
        functools.partial(sum_body, 2, NX, NY * WROWS),
        shape((NX, NY * WROWS + SMALL, 128), BF),
        [VM],
    )(got)
    got = lax.all_to_all(got, "dp", 0, 0, tiled=True, axis_index_groups=XS)
    got = call(
        functools.partial(sum_body, NX, NY, WROWS), shape((NY, WROWS + SMALL, 128), BF), [VM]
    )(got)
    got = lax.all_to_all(got, "dp", 0, 0, tiled=True, axis_index_groups=YS)
    got = call(last_sum_body, shape((8, WROWS + SMALL, 128), BF), [VM])(got)
    got = lax.all_to_all(got, ("gy", "gx"), 0, 0, tiled=True, axis_index_groups=ZS)
    mine, small = call(z_body, [shape((WROWS, 128), BF), shape((8, 128), F32)], [VM])(got)
    theirs = lax.ppermute(mine, "gy", [(0, 1), (1, 0), (2, 3), (3, 2)])
    grad_qkv, grad_out, grad_gain, grad_bias = call(
        finish_body,
        [
            shape((16, 3 * INNER), F32),
            shape((8, D), F32),
            shape((1, D), F32),
            shape((HEADS, 49), F32),
        ],
        [SM, VM, VM, VM],
    )(place, mine, theirs, small)
    return (
        update.reshape(tokens.shape),
        grad_tokens.reshape(tokens.shape),
        grad_qkv,
        grad_out,
        grad_gain.reshape(D),
        grad_bias,
    )


def solution(mesh):
    return jax.shard_map(
        shards,
        mesh=mesh,
        in_specs=(
            P("dp", "gy", "gx", None, None),
            P("dp", None, None, None),
            P("dp", None),
            P("dp", None),
            P(),
            P(),
            P("dp", "gy", "gx", None, None),
        ),
        out_specs=(
            P("dp", "gy", "gx", None, None),
            P("dp", "gy", "gx", None, None),
            P("dp", None),
            P("dp", None),
            P(),
            P(),
        ),
        check_vma=False,
    )
```

```python
import functools

import jax
import jax.numpy as jnp
from jax import lax
from jax.experimental import pallas as pl
from jax.experimental.pallas import tpu as pltpu
from jax.sharding import PartitionSpec as P

D = 512
HEADS = 8
HD = 32
INNER = 256
TILE = 8
HALO = 3
REG = 4
CAP = 2
ROWS = 128
CELLS = TILE * TILE
DP = 32
NX = 4
NY = 8
PAIRS = 7
TILES = PAIRS * 2
BROWS = HEADS * CELLS
T_ROWS = 48
G_ROWS = 32
STRIP = T_ROWS + G_ROWS
MESSAGE = 2 * ROWS + 2 * STRIP
CHUNK = 128
FAR = 9
SCALE = HD ** (-0.5)
WROWS = 64
SMALL = 16
CORES = [[0, 1], [2, 3]]
XS = [[x * NY + y for x in range(NX)] for y in range(NY)]
YS = [[x * NY + y for y in range(NY)] for x in range(NX)]
ZS = [[0, 1, 2, 3, 8, 9, 10, 11], [4, 5, 6, 7, 12, 13, 14, 15]]
F32 = jnp.float32
BF = jnp.bfloat16
NT = (((1,), (1,)), ((), ()))
TN = (((0,), (0,)), ((), ()))
VM = pl.BlockSpec(memory_space=pltpu.VMEM)
SM = pl.BlockSpec(memory_space=pltpu.SMEM)
HBM = pl.BlockSpec(memory_space=pltpu.HBM)


def dot(a, b, dims=(((1,), (0,)), ((), ()))):
    return lax.dot_general(a, b, dims, preferred_element_type=F32)


def call(body, outs, ins, scratch=(), limit=16, flops=1000000, traffic=1000000):
    single = not isinstance(outs, (list, tuple))
    return pl.pallas_call(
        body,
        out_shape=outs,
        in_specs=ins,
        out_specs=VM if single else [VM] * len(outs),
        scratch_shapes=list(scratch),
        compiler_params=pltpu.CompilerParams(vmem_limit_bytes=limit * 2**20),
        cost_estimate=pl.CostEstimate(flops=flops, bytes_accessed=traffic, transcendentals=0),
    )


def shape(dims, dtype):
    return jax.ShapeDtypeStruct(dims, dtype)


def pack_body(wq_in, wo_in, tok_in, grad_in, w_out, rows, near, far, wq, wo, sems):
    even = lax.axis_index("gy") % 2 == 0
    copies = [
        pltpu.make_async_copy(wq_in, wq, sems.at[0]),
        pltpu.make_async_copy(wo_in, wo, sems.at[1]),
        pltpu.make_async_copy(tok_in, rows.at[pl.ds(0, ROWS)], sems.at[2]),
        pltpu.make_async_copy(grad_in, rows.at[pl.ds(ROWS, ROWS)], sems.at[3]),
    ]
    for copy in copies:
        copy.start()
    copies[0].wait()
    copies[1].wait()

    def half(c):
        parts = [wq[:, (3 * c + j) * 128 : (3 * c + j + 1) * 128].astype(F32) for j in range(3)]
        parts += [wo[:, (2 * c + j) * 128 : (2 * c + j + 1) * 128].astype(F32) for j in range(2)]
        block = jnp.concatenate(parts, axis=0).astype(BF)
        for d in range(DP):
            w_out[d] = block

    pl.when(even)(lambda: half(0))
    pl.when(jnp.logical_not(even))(lambda: half(1))
    copies[2].wait()
    copies[3].wait()

    def strips(down, up):
        for s in range(CAP):
            t, g = s * CELLS, ROWS + s * CELLS
            down[s, 0:T_ROWS, :] = rows[t + CELLS - T_ROWS : t + CELLS, :]
            down[s, T_ROWS:STRIP, :] = rows[g + CELLS - G_ROWS : g + CELLS, :]
            up[s, 0:T_ROWS, :] = rows[t : t + T_ROWS, :]
            up[s, T_ROWS:STRIP, :] = rows[g : g + G_ROWS, :]

    pl.when(even)(lambda: strips(near, far))
    pl.when(jnp.logical_not(even))(lambda: strips(far, near))


def corner_body(place, tiles, rows, near, far, first, second, local):
    local[0 : 2 * ROWS, :] = rows[...]
    row, col = place[0], place[1]
    over = jnp.maximum(row - 1, 0)
    under = jnp.minimum(row + 1, 3)

    def build(above, below, to_right, to_left):
        for n, strips in enumerate((above, below)):
            for s in range(CAP):
                at = 2 * ROWS + (2 * n + s) * STRIP
                local[at : at + STRIP, :] = strips[s]
        for out, top, bottom in ((to_right, 15, 3), (to_left, 12, 0)):
            out[0 : 2 * ROWS, :] = rows[...]
            out[2 * ROWS : 2 * ROWS + STRIP, :] = above[
                (tiles[over, col, 1] == top).astype(jnp.int32)
            ]
            out[2 * ROWS + STRIP : MESSAGE, :] = below[
                (tiles[under, col, 1] == bottom).astype(jnp.int32)
            ]

    for odd_row in range(2):
        for odd_col in range(2):
            here = ((row & 1) == odd_row) & ((col & 1) == odd_col)
            rows_of = (near, far) if odd_row else (far, near)
            outs = (second, first) if odd_col else (first, second)
            pl.when(here)(functools.partial(build, *rows_of, *outs))


def plan_tiles(place, tiles, plan, crow, ccol):
    my_row, my_col = place[0], place[1]
    side = 1 - 2 * (my_col & 1)
    steps = [(0, 0)] * 2 + [(-1, 0)] * 2 + [(1, 0)] * 2 + [(0, side)] * 2 + [(0, -side)] * 2
    even = side > 0
    corners = [
        (-1, side, jnp.where(even, 12, 15)),
        (-1, -side, jnp.where(even, 15, 12)),
        (1, side, jnp.where(even, 0, 3)),
        (1, -side, jnp.where(even, 3, 0)),
    ]
    for t, (dy, dx, *corner) in enumerate(steps + corners):
        ry, rx = my_row + dy, my_col + dx
        there = (ry >= 0) & (ry < 4) & (rx >= 0) & (rx < 4)
        ty, tx = jnp.clip(ry, 0, 3), jnp.clip(rx, 0, 3)
        if corner:
            tile = corner[0]
            there = there & ((tiles[ty, tx, 0] == tile) | (tiles[ty, tx, 1] == tile))
        else:
            tile = tiles[ty, tx, t % 2]
        crow[t] = jnp.where(there, ry * REG + (tile >> 2), -1000 * (t + 1))
        ccol[t] = jnp.where(there, rx * REG + (tile & 3), -1000 * (t + 1))

    def near(a, b):
        return (jnp.abs(crow[a] - crow[b]) <= 1) & (jnp.abs(ccol[a] - ccol[b]) <= 1)

    def tile_plan(t, carry):
        plan[t, 0] = (near(t, 0) | near(t, 1)).astype(jnp.int32)
        count = jnp.int32(0)
        for r in range(PAIRS):
            plan[t, 2 + count] = r
            both = jnp.int32(0)
            for s in range(2):
                k = 2 * r + s
                close = near(t, k)
                down, across = crow[k] - crow[t], ccol[k] - ccol[t]
                plan[t, 10 + 8 * s + count] = jnp.where(close, down * 3 + across + 4, FAR)
                plan[t, 26 + 8 * s + count] = jnp.where(
                    close, (64 * down + 8 * across + 512) & 127, 0
                )
                both = both | close.astype(jnp.int32)
            count = count + both
        plan[t, 1] = count
        return carry

    lax.fori_loop(0, TILES, tile_plan, 0)
    plan[0, 47] = my_row & 1


def bias_tables(base_ref, tab):
    query = lax.broadcasted_iota(jnp.int32, (CELLS, 128), 0)
    lane = lax.broadcasted_iota(jnp.int32, (CELLS, 128), 1)
    key = lane & 63
    left = lane < 64
    row_step = (key >> 3) - (query >> 3)
    col_step = (key & 7) - (query & 7)
    base = base_ref[...]
    for place in range(9):
        down, across = place // 3 - 1, place % 3 - 1
        shift = 64 * down + 8 * across
        inside = (jnp.abs(row_step + 8 * down) <= HALO) & (jnp.abs(col_step + 8 * across) <= HALO)
        first = pltpu.roll(base, (-shift - 27) % 128, 1)
        second = pltpu.roll(base, (64 - shift - 27) % 128, 1)
        for h in range(HEADS):
            a = pltpu.roll(
                jnp.broadcast_to(first[h : h + 1], (CELLS, 128)), 0, 1, stride=1, stride_axis=0
            )
            b = pltpu.roll(
                jnp.broadcast_to(second[h : h + 1], (CELLS, 128)), 0, 1, stride=1, stride_axis=0
            )
            tab[place, h * CELLS : (h + 1) * CELLS, :] = jnp.where(
                inside, jnp.where(left, a, b), -jnp.inf
            )
    tab[FAR] = jnp.full((BROWS, 128), -jnp.inf, F32)


def prepare(local, left, right, gain, out):
    normed = out.at[pl.ds(0, PAIRS * ROWS)]
    grads = out.at[pl.ds(PAIRS * ROWS, PAIRS * ROWS)]
    own = out.at[pl.ds(2 * PAIRS * ROWS, ROWS)]
    gain_row = gain[...]

    def norm(block):
        x = block.astype(F32)
        inv = lax.rsqrt(jnp.mean(x * x, axis=-1, keepdims=True) + 1e-06)
        return (x * inv * gain_row).astype(BF)

    own[...] = local[0:ROWS, :]
    for t, source in ((0, local), (6, left), (8, right)):
        at = t * CELLS
        normed[at : at + ROWS, :] = norm(source[0:ROWS, :])
        grads[at : at + ROWS, :] = source[ROWS : 2 * ROWS, :]
    at_a, at_b, at_c = 2 * ROWS, 2 * ROWS + STRIP, 2 * ROWS + 2 * STRIP
    upper = [
        (2, local[at_a : at_a + STRIP, :]),
        (3, local[at_b : at_b + STRIP, :]),
        (10, left[at_a : at_a + STRIP, :]),
        (11, right[at_a : at_a + STRIP, :]),
    ]
    lower = [
        (4, local[at_c : at_c + STRIP, :]),
        (5, local[at_c + STRIP : at_c + 2 * STRIP, :]),
        (12, left[at_b : at_b + STRIP, :]),
        (13, right[at_b : at_b + STRIP, :]),
    ]
    for t, strip in upper:
        at = t * CELLS
        normed[at : at + CELLS - T_ROWS, :] = jnp.zeros((CELLS - T_ROWS, D), BF)
        normed[at + CELLS - T_ROWS : at + CELLS, :] = norm(strip[0:T_ROWS])
        grads[at : at + CELLS - G_ROWS, :] = jnp.zeros((CELLS - G_ROWS, D), BF)
        grads[at + CELLS - G_ROWS : at + CELLS, :] = strip[T_ROWS:STRIP]
    for t, strip in lower:
        at = t * CELLS
        normed[at : at + T_ROWS, :] = norm(strip[0:T_ROWS])
        normed[at + T_ROWS : at + CELLS, :] = jnp.zeros((CELLS - T_ROWS, D), BF)
        grads[at : at + G_ROWS, :] = strip[T_ROWS:STRIP]
        grads[at + G_ROWS : at + CELLS, :] = jnp.zeros((CELLS - G_ROWS, D), BF)


def main_body(
    plan,
    local,
    first,
    second,
    w_mine,
    w_other,
    gain,
    base,
    update,
    grad_tokens,
    sums,
    wq,
    wo,
    qkv,
    gatt,
    qbd,
    gbd,
    scores,
    dprobs,
    top,
    total,
    delta,
    pbf,
    dsf,
    att,
    dq,
    attended,
    dqkv,
    dk,
    dv,
    hist,
    rowsum,
    packed,
    tab,
):
    bias_tables(base, tab)
    prepare(local, first, second, gain, packed)
    normed = packed.at[pl.ds(0, PAIRS * ROWS)]
    grads = packed.at[pl.ds(PAIRS * ROWS, PAIRS * ROWS)]
    tokens = packed.at[pl.ds(2 * PAIRS * ROWS, ROWS)]
    core = plan[0, 47]
    for c, part in ((core, w_mine), (1 - core, w_other)):
        for j in range(3):
            wq[3 * c + j] = part[:, 16 * j : 16 * j + 16, :].reshape(D, 128)
        both = part[:, 48:64, :].astype(F32)
        for j in range(2):
            wo[2 * c + j] = both[:, 8 * j : 8 * j + 8, :].reshape(INNER, 128).astype(BF)

    def columns(blocks, first, last):
        return jnp.concatenate([blocks[j] for j in range(first, last)], axis=1)

    gain_row = gain[...]
    for j in range(3):
        cols = slice(j * INNER, (j + 1) * INNER)
        qkv[:, cols] = dot(normed[...], columns(wq, 2 * j, 2 * j + 2)).astype(BF)
    gatt[...] = dot(grads[...], columns(wo, 0, 4), NT).astype(BF)

    dk[...] = jnp.zeros_like(dk)
    dv[...] = jnp.zeros_like(dv)
    hist[...] = jnp.zeros_like(hist)
    head_of = lax.broadcasted_iota(jnp.int32, (1, INNER), 1) >> 5
    masks_bf = [(head_of == h).astype(F32).astype(BF) for h in range(HEADS)]
    lane = lax.broadcasted_iota(jnp.int32, (CHUNK, 128), 1)
    first_slot = lane < 64
    lane_masks = [((lane[0:CELLS] >> 5) == h).astype(F32) for h in range(4)]
    mirror = ((lane + lax.broadcasted_iota(jnp.int32, (128, 128), 0)) == 127).astype(F32)
    mirror_bf = mirror.astype(BF)

    def process(i, own, q_at, nq):
        per = CHUNK // nq
        chunks = HEADS // per
        used = HEADS * nq
        at = pl.multiple_of(i * CELLS, CELLS) + q_at
        queries = qkv[pl.ds(at, nq), 0:INNER]
        cotangents = gatt[pl.ds(at, nq), :]
        for h in range(HEADS):
            qbd[h * nq : (h + 1) * nq, :] = queries * masks_bf[h]
            gbd[h * nq : (h + 1) * nq, :] = cotangents * masks_bf[h]
        count = plan[i, 1]

        def bias_of(off, c):
            parts = [
                tab[off, (c * per + h) * CELLS + q_at : (c * per + h) * CELLS + q_at + nq, :]
                for h in range(per)
            ]
            return jnp.concatenate(parts, axis=0)

        def pass_a(b, first):
            k_at = pl.multiple_of(plan[i, 2 + b] * ROWS, ROWS)
            keys = qkv[pl.ds(k_at, ROWS), INNER : 2 * INNER]
            values = qkv[pl.ds(k_at, ROWS), 2 * INNER : 3 * INNER]
            off_a, off_b = plan[i, 10 + b], plan[i, 18 + b]
            scores[b, 0:used, :] = dot(qbd[0:used, :], keys, NT)
            dprobs[b, 0:used, :] = dot(gbd[0:used, :], values, NT)
            for c in range(chunks):
                rows = slice(c * CHUNK, (c + 1) * CHUNK)
                bias = jnp.where(first_slot, bias_of(off_a, c), bias_of(off_b, c))
                s = scores[b, rows, :] * SCALE + bias
                scores[b, rows, :] = s
                top[rows, :] = s if first else jnp.maximum(top[rows, :], s)

        def rest_a(b, carry):
            pass_a(b, False)
            return carry

        pass_a(0, True)
        lax.fori_loop(1, count, rest_a, 0)
        for c in range(chunks):
            rows = slice(c * CHUNK, (c + 1) * CHUNK)
            top[rows, :] = jnp.broadcast_to(
                jnp.max(top[rows, :], axis=-1, keepdims=True), (CHUNK, 128)
            )

        def pass_b(b, first):
            for c in range(chunks):
                rows = slice(c * CHUNK, (c + 1) * CHUNK)
                e = jnp.exp(scores[b, rows, :] - top[rows, :])
                d = e * dprobs[b, rows, :]
                scores[b, rows, :] = e
                total[rows, :] = e if first else total[rows, :] + e
                delta[rows, :] = d if first else delta[rows, :] + d

        def rest_b(b, carry):
            pass_b(b, False)
            return carry

        pass_b(0, True)
        lax.fori_loop(1, count, rest_b, 0)
        for c in range(chunks):
            rows = slice(c * CHUNK, (c + 1) * CHUNK)
            inverse = 1.0 / jnp.sum(total[rows, :], axis=-1, keepdims=True)
            d = jnp.sum(delta[rows, :], axis=-1, keepdims=True) * inverse
            total[rows, :] = jnp.broadcast_to(inverse, (CHUNK, 128))
            delta[rows, :] = jnp.broadcast_to(d, (CHUNK, 128))

        def probs_of(b):
            for c in range(chunks):
                rows = slice(c * CHUNK, (c + 1) * CHUNK)
                p = scores[b, rows, :] * total[rows, :]
                pbf[rows, :] = p.astype(BF)
                dsf[rows, :] = (p * (dprobs[b, rows, :] - delta[rows, :])).astype(BF)

        def pass_c(b, first):
            k_at = pl.multiple_of(plan[i, 2 + b] * ROWS, ROWS)
            keys = qkv[pl.ds(k_at, ROWS), INNER : 2 * INNER]
            values = qkv[pl.ds(k_at, ROWS), 2 * INNER : 3 * INNER]
            probs_of(b)
            for sum_ref, factor, other in ((att, pbf, values), (dq, dsf, keys)):
                wide = dot(factor[...], other)
                for n in range(2):
                    cols = slice(n * 128, (n + 1) * 128)
                    acc = None if first else sum_ref[:, cols]
                    for h in range(4 * n, 4 * n + 4):
                        part = wide[h * CELLS : (h + 1) * CELLS, cols] * lane_masks[h & 3]
                        acc = part if acc is None else acc + part
                    sum_ref[:, cols] = acc
            flipped = dot(dsf[...], mirror_bf)
            half = first_slot[0:CELLS]
            for h in range(HEADS):
                ds = flipped[h * CELLS : (h + 1) * CELLS]
                for s, part in enumerate((jnp.where(half, 0.0, ds), jnp.where(half, ds, 0.0))):
                    turned = pltpu.roll(part, 0, 1, stride=1, stride_axis=0)
                    rowsum[s, h : h + 1, :] = jnp.sum(turned, axis=0, keepdims=True)
            for s in range(2):
                shift = (64 * s - 27 - plan[i, 26 + 8 * s + b] + 256) & 127
                hist[...] += pltpu.roll(rowsum[s], shift, 1)

        def rest_c(b, carry):
            pass_c(b, False)
            return carry

        if own:
            pass_c(0, True)
        else:
            probs_of(0)
        dk[...] += dot(dsf[0:used, :], qbd[0:used, :], TN)
        dv[...] += dot(pbf[0:used, :], gbd[0:used, :], TN)
        if own:
            lax.fori_loop(1, count, rest_c, 0)
            slot_at = pl.multiple_of(i * CELLS, CELLS)
            attended[pl.ds(slot_at, CELLS), :] = att[...].astype(BF)
            dqkv[pl.ds(slot_at, CELLS), 0:INNER] = (dq[...] * SCALE).astype(BF)

    def own_step(s, carry):
        process(s, True, 0, CELLS)
        return carry

    lax.fori_loop(0, 2, own_step, 0)

    def others(tile_of, q_at, nq):
        def step(n, carry):
            t = tile_of(n)
            pl.when(plan[t, 0] > 0)(lambda: process(t, False, q_at, nq))
            return carry

        lax.fori_loop(0, 4, step, 0)

    others(lambda n: n + 6, 0, CELLS)
    others(lambda n: n + jnp.where(n < 2, 2, 8), CELLS - G_ROWS, G_ROWS)
    others(lambda n: n + jnp.where(n < 2, 4, 10), 0, G_ROWS)

    dqkv[:, INNER : 2 * INNER] = (dk[...] * SCALE).astype(BF)
    dqkv[:, 2 * INNER : 3 * INNER] = dv[...].astype(BF)
    update[...] = dot(attended[...], columns(wo, 0, 4)).astype(BF)
    grad_out = dot(attended[...], grads[0:ROWS, :], TN)
    for c in range(2):
        pair = [
            grad_out[:, (2 * c + j) * 128 : (2 * c + j + 1) * 128].reshape(DP, 8, 128)
            for j in range(2)
        ]
        both = jnp.concatenate(pair, axis=1).astype(BF)
        for d in range(DP):
            sums[c, d * WROWS + 48 : d * WROWS + 64, :] = both[d]
    for n in range(3):
        pair = dot(normed[0:ROWS, :], dqkv[:, n * 256 : (n + 1) * 256], TN).astype(BF)
        for j in (2 * n, 2 * n + 1):
            block = pair[:, (j - 2 * n) * 128 : (j - 2 * n + 1) * 128]
            for d in range(DP):
                at = d * WROWS + (j % 3) * 16
                sums[j // 3, at : at + 16, :] = block[d * 16 : (d + 1) * 16]
    d_normed = dot(dqkv[...], columns(wq, 0, 6), NT)
    x = tokens[...].astype(F32)
    inv = lax.rsqrt(jnp.mean(x * x, axis=-1, keepdims=True) + 1e-06)
    scaled = d_normed * gain_row
    gain_sum = jnp.sum(d_normed * x * inv, axis=0, keepdims=True)
    grad_tokens[...] = (
        inv * scaled - x * (inv * inv * inv) * jnp.mean(scaled * x, axis=-1, keepdims=True)
    ).astype(BF)
    offsets = lax.dot_general(
        hist[...],
        mirror,
        (((1,), (0,)), ((), ())),
        precision=lax.Precision.HIGHEST,
        preferred_element_type=F32,
    )
    folded = offsets[0:4, :] + pltpu.roll(offsets[4:8, :], 64, 1)
    small = jnp.concatenate([gain_sum[:, j * 128 : (j + 1) * 128] for j in range(4)] + [folded], 0)
    split = halves(small)
    sums[0, DP * WROWS : DP * WROWS + SMALL, :] = split
    sums[1, DP * WROWS : DP * WROWS + SMALL, :] = split


def halves(value):
    high = value.astype(BF).astype(F32)
    return jnp.concatenate([high, value - high], axis=0).astype(BF)


def whole(value):
    wide = value.astype(F32)
    return wide[..., 0:8, :] + wide[..., 8:16, :]


def sum_body(senders, parts, span, received, out):
    rows = parts * span
    for p in range(parts):
        acc = received[0, p * span : (p + 1) * span, :].astype(F32)
        for s in range(1, senders):
            acc += received[s, p * span : (p + 1) * span, :].astype(F32)
        out[p, 0:span, :] = acc.astype(BF)
    small = whole(received[0, rows : rows + SMALL, :])
    for s in range(1, senders):
        small += whole(received[s, rows : rows + SMALL, :])
    split = halves(small)
    for p in range(parts):
        out[p, span : span + SMALL, :] = split


def last_sum_body(received, out):
    acc = received[0, 0:WROWS, :].astype(F32)
    small = whole(received[0, WROWS : WROWS + SMALL, :])
    for s in range(1, NY):
        acc += received[s, 0:WROWS, :].astype(F32)
        small += whole(received[s, WROWS : WROWS + SMALL, :])
    acc = acc.astype(BF)
    split = halves(small)
    for p in range(8):
        out[p, 0:WROWS, :] = acc
        out[p, WROWS : WROWS + SMALL, :] = split


def z_body(received, mine, small):
    acc = received[0, 0:WROWS, :].astype(F32)
    more = whole(received[0, WROWS : WROWS + SMALL, :])
    for s in range(1, 8):
        acc += received[s, 0:WROWS, :].astype(F32)
        more += whole(received[s, WROWS : WROWS + SMALL, :])
    mine[...] = acc.astype(BF)
    small[...] = more


def finish_body(place, mine, theirs, small_in, grad_qkv, grad_out, grad_gain, grad_bias):
    small = small_in[...]
    odd = place[0] & 1

    def unpack(pair):
        for c, ref in enumerate(pair):
            acc = ref[...].astype(F32)
            for j in range(3):
                at = (3 * c + j) * 128
                grad_qkv[:, at : at + 128] = acc[16 * j : 16 * j + 16, :]
            for j in range(2):
                at = 48 + 8 * j
                grad_out[:, (2 * c + j) * 128 : (2 * c + j + 1) * 128] = acc[at : at + 8, :]

    pl.when(odd == 0)(lambda: unpack((mine, theirs)))
    pl.when(odd == 1)(lambda: unpack((theirs, mine)))
    for j in range(4):
        grad_gain[:, j * 128 : (j + 1) * 128] = small[j : j + 1, :]
    folded = small[4:8, :]
    table = jnp.concatenate([folded, pltpu.roll(folded, 64, 1)], axis=0)
    lane = lax.broadcasted_iota(jnp.int32, (HEADS, 128), 1)
    out = jnp.zeros((HEADS, 128), F32)
    for r in range(7):
        moved = table if r == 0 else pltpu.roll(table, 128 - r, 1)
        out = jnp.where((lane >= 7 * r) & (lane < 7 * r + 7), moved, out)
    grad_bias[...] = out[:, 0:49]


def layer(plan, local, first, second, w_mine, w_other, gain, base):
    f32 = lambda *dims: pltpu.VMEM(dims, F32)
    bf = lambda *dims: pltpu.VMEM(dims, BF)
    return call(
        main_body,
        [
            shape((ROWS, D), BF),
            shape((ROWS, D), BF),
            shape((2, DP * WROWS + SMALL, 128), BF),
        ],
        [SM] + [VM] * 7,
        [
            bf(6, D, 128),
            bf(4, INNER, 128),
            bf(PAIRS * ROWS, 3 * INNER),
            bf(PAIRS * ROWS, INNER),
            bf(BROWS, INNER),
            bf(BROWS, INNER),
            f32(4, BROWS, 128),
            f32(4, BROWS, 128),
            f32(BROWS, 128),
            f32(BROWS, 128),
            f32(BROWS, 128),
            bf(BROWS, 128),
            bf(BROWS, 128),
            f32(CELLS, INNER),
            f32(CELLS, INNER),
            bf(ROWS, INNER),
            bf(ROWS, 3 * INNER),
            f32(ROWS, INNER),
            f32(ROWS, INNER),
            f32(HEADS, 128),
            f32(CAP, HEADS, 128),
            bf(2 * PAIRS * ROWS + ROWS, D),
            f32(FAR + 1, BROWS, 128),
        ],
        limit=40,
        flops=4000000000,
        traffic=12000000,
    )(plan, local, first, second, w_mine, w_other, gain, base)


def shards(tokens, tile_ids, w_qkv, w_out, norm_gain, rel_bias, update_grad):
    my_row = lax.axis_index("gy")
    my_col = lax.axis_index("gx")
    place = jnp.stack([my_row, my_col]).astype(jnp.int32)
    pairs = [(0, 1), (1, 0), (2, 3), (3, 2)]
    middle = [(1, 2), (2, 1)]

    tiles = tile_ids.reshape(4, 4, CAP)
    strip = shape((CAP, STRIP, D), BF)
    w_send, rows, near, far = call(
        pack_body,
        [shape((DP, WROWS, 128), BF), shape((2 * ROWS, D), BF), strip, strip],
        [HBM, HBM, HBM, HBM],
        [
            pltpu.VMEM((16, 3 * INNER), BF),
            pltpu.VMEM((8, D), BF),
            pltpu.SemaphoreType.DMA((4,)),
        ],
        limit=60,
    )(w_qkv, w_out, tokens.reshape(ROWS, D), update_grad.reshape(ROWS, D))
    near = lax.ppermute(near, "gy", pairs)
    far = lax.ppermute(far, "gy", middle)
    w_mine = lax.all_to_all(w_send, "dp", 0, 0, tiled=True)
    message = shape((MESSAGE, D), BF)
    stays = shape((2 * ROWS + 4 * STRIP, D), BF)
    first, second, local = call(
        corner_body, [message, message, stays], [SM, SM, VM, VM, VM], flops=16000000000
    )(place, tiles, rows, near, far)
    first = lax.ppermute(first, "gx", pairs)
    second = lax.ppermute(second, "gx", middle)
    base = jnp.pad(rel_bias.reshape(HEADS, 7, 7), ((0, 0), (0, 0), (0, 1))).reshape(HEADS, 56)
    base = jnp.pad(base, ((0, 0), (0, 72)))
    plan = pl.pallas_call(
        plan_tiles,
        out_shape=shape((TILES, 48), jnp.int32),
        in_specs=[SM, SM],
        out_specs=SM,
        scratch_shapes=[pltpu.SMEM((TILES,), jnp.int32), pltpu.SMEM((TILES,), jnp.int32)],
        cost_estimate=pl.CostEstimate(flops=2000000, bytes_accessed=4000000, transcendentals=0),
    )(place, tiles)
    w_mine = lax.optimization_barrier((w_mine, first, second, plan))[0]
    w_other = lax.ppermute(w_mine, "gy", pairs)

    update, grad_tokens, sums = layer(
        plan, local, first, second, w_mine, w_other, norm_gain.reshape(1, D), base
    )

    got = lax.all_to_all(sums, "gy", 0, 0, tiled=True, axis_index_groups=CORES)
    got = call(
        functools.partial(sum_body, 2, NX, NY * WROWS),
        shape((NX, NY * WROWS + SMALL, 128), BF),
        [VM],
    )(got)
    got = lax.all_to_all(got, "dp", 0, 0, tiled=True, axis_index_groups=XS)
    got = call(
        functools.partial(sum_body, NX, NY, WROWS), shape((NY, WROWS + SMALL, 128), BF), [VM]
    )(got)
    got = lax.all_to_all(got, "dp", 0, 0, tiled=True, axis_index_groups=YS)
    got = call(last_sum_body, shape((8, WROWS + SMALL, 128), BF), [VM])(got)
    got = lax.all_to_all(got, ("gy", "gx"), 0, 0, tiled=True, axis_index_groups=ZS)
    mine, small = call(z_body, [shape((WROWS, 128), BF), shape((8, 128), F32)], [VM])(got)
    theirs = lax.ppermute(mine, "gy", pairs)
    grad_qkv, grad_out, grad_gain, grad_bias = call(
        finish_body,
        [
            shape((16, 3 * INNER), F32),
            shape((8, D), F32),
            shape((1, D), F32),
            shape((HEADS, 49), F32),
        ],
        [SM, VM, VM, VM],
    )(place, mine, theirs, small)
    return (
        update.reshape(tokens.shape),
        grad_tokens.reshape(tokens.shape),
        grad_qkv,
        grad_out,
        grad_gain.reshape(D),
        grad_bias,
    )


def solution(mesh):
    return jax.shard_map(
        shards,
        mesh=mesh,
        in_specs=(
            P("dp", "gy", "gx", None, None),
            P("dp", None, None, None),
            P("dp", None),
            P("dp", None),
            P(),
            P(),
            P("dp", "gy", "gx", None, None),
        ),
        out_specs=(
            P("dp", "gy", "gx", None, None),
            P("dp", "gy", "gx", None, None),
            P("dp", None),
            P("dp", None),
            P(),
            P(),
        ),
        check_vma=False,
    )
```

```python
import functools

import jax
import jax.numpy as jnp
from jax import lax
from jax.experimental import pallas as pl
from jax.experimental.pallas import tpu as pltpu
from jax.sharding import PartitionSpec as P

D = 512
HEADS = 8
HD = 32
INNER = 256
TILE = 8
HALO = 3
REG = 4
CAP = 2
ROWS = 128
CELLS = TILE * TILE
DP = 32
NX = 4
NY = 8
PAIRS = 7
TILES = PAIRS * 2
BROWS = HEADS * CELLS
T_ROWS = 48
G_ROWS = 32
STRIP = T_ROWS + G_ROWS
MESSAGE = 2 * ROWS + 2 * STRIP
CHUNK = 128
FAR = 9
SCALE = HD ** (-0.5)
WROWS = 64
SMALL = 16
CORES = [[0, 1], [2, 3]]
XS = [[x * NY + y for x in range(NX)] for y in range(NY)]
YS = [[x * NY + y for y in range(NY)] for x in range(NX)]
ZS = [[0, 1, 2, 3, 8, 9, 10, 11], [4, 5, 6, 7, 12, 13, 14, 15]]
F32 = jnp.float32
BF = jnp.bfloat16
NT = (((1,), (1,)), ((), ()))
TN = (((0,), (0,)), ((), ()))
VM = pl.BlockSpec(memory_space=pltpu.VMEM)
SM = pl.BlockSpec(memory_space=pltpu.SMEM)
HBM = pl.BlockSpec(memory_space=pltpu.HBM)


def dot(a, b, dims=(((1,), (0,)), ((), ()))):
    return lax.dot_general(a, b, dims, preferred_element_type=F32)


def call(body, outs, ins, scratch=(), limit=16, flops=1000000, traffic=1000000):
    single = not isinstance(outs, (list, tuple))
    return pl.pallas_call(
        body,
        out_shape=outs,
        in_specs=ins,
        out_specs=VM if single else [VM] * len(outs),
        scratch_shapes=list(scratch),
        compiler_params=pltpu.CompilerParams(vmem_limit_bytes=limit * 2**20),
        cost_estimate=pl.CostEstimate(flops=flops, bytes_accessed=traffic, transcendentals=0),
    )


def shape(dims, dtype):
    return jax.ShapeDtypeStruct(dims, dtype)


def pack_body(wq_in, wo_in, tok_in, grad_in, w_out, rows, near, far, wq, wo, sems):
    even = lax.axis_index("gy") % 2 == 0
    copies = [
        pltpu.make_async_copy(wq_in, wq, sems.at[0]),
        pltpu.make_async_copy(wo_in, wo, sems.at[1]),
        pltpu.make_async_copy(tok_in, rows.at[pl.ds(0, ROWS)], sems.at[2]),
        pltpu.make_async_copy(grad_in, rows.at[pl.ds(ROWS, ROWS)], sems.at[3]),
    ]
    for copy in copies:
        copy.start()
    copies[0].wait()
    copies[1].wait()

    def half(c):
        parts = [wq[:, (3 * c + j) * 128 : (3 * c + j + 1) * 128].astype(F32) for j in range(3)]
        parts += [wo[:, (2 * c + j) * 128 : (2 * c + j + 1) * 128].astype(F32) for j in range(2)]
        block = jnp.concatenate(parts, axis=0).astype(BF)
        for d in range(DP):
            w_out[d] = block

    pl.when(even)(lambda: half(0))
    pl.when(jnp.logical_not(even))(lambda: half(1))
    copies[2].wait()
    copies[3].wait()

    def strips(down, up):
        for s in range(CAP):
            t, g = s * CELLS, ROWS + s * CELLS
            down[s, 0:T_ROWS, :] = rows[t + CELLS - T_ROWS : t + CELLS, :]
            down[s, T_ROWS:STRIP, :] = rows[g + CELLS - G_ROWS : g + CELLS, :]
            up[s, 0:T_ROWS, :] = rows[t : t + T_ROWS, :]
            up[s, T_ROWS:STRIP, :] = rows[g : g + G_ROWS, :]

    pl.when(even)(lambda: strips(near, far))
    pl.when(jnp.logical_not(even))(lambda: strips(far, near))


def corner_body(place, tiles, rows, near, far, first, second, local):
    local[0 : 2 * ROWS, :] = rows[...]
    row, col = place[0], place[1]
    over = jnp.maximum(row - 1, 0)
    under = jnp.minimum(row + 1, 3)

    def build(above, below, to_right, to_left):
        for n, strips in enumerate((above, below)):
            for s in range(CAP):
                at = 2 * ROWS + (2 * n + s) * STRIP
                local[at : at + STRIP, :] = strips[s]
        for out, top, bottom in ((to_right, 15, 3), (to_left, 12, 0)):
            out[0 : 2 * ROWS, :] = rows[...]
            out[2 * ROWS : 2 * ROWS + STRIP, :] = above[
                (tiles[over, col, 1] == top).astype(jnp.int32)
            ]
            out[2 * ROWS + STRIP : MESSAGE, :] = below[
                (tiles[under, col, 1] == bottom).astype(jnp.int32)
            ]

    for odd_row in range(2):
        for odd_col in range(2):
            here = ((row & 1) == odd_row) & ((col & 1) == odd_col)
            rows_of = (near, far) if odd_row else (far, near)
            outs = (second, first) if odd_col else (first, second)
            pl.when(here)(functools.partial(build, *rows_of, *outs))


def plan_tiles(place, tiles, plan, crow, ccol):
    my_row, my_col = place[0], place[1]
    side = 1 - 2 * (my_col & 1)
    steps = [(0, 0)] * 2 + [(-1, 0)] * 2 + [(1, 0)] * 2 + [(0, side)] * 2 + [(0, -side)] * 2
    even = side > 0
    corners = [
        (-1, side, jnp.where(even, 12, 15)),
        (-1, -side, jnp.where(even, 15, 12)),
        (1, side, jnp.where(even, 0, 3)),
        (1, -side, jnp.where(even, 3, 0)),
    ]
    for t, (dy, dx, *corner) in enumerate(steps + corners):
        ry, rx = my_row + dy, my_col + dx
        there = (ry >= 0) & (ry < 4) & (rx >= 0) & (rx < 4)
        ty, tx = jnp.clip(ry, 0, 3), jnp.clip(rx, 0, 3)
        if corner:
            tile = corner[0]
            there = there & ((tiles[ty, tx, 0] == tile) | (tiles[ty, tx, 1] == tile))
        else:
            tile = tiles[ty, tx, t % 2]
        crow[t] = jnp.where(there, ry * REG + (tile >> 2), -1000 * (t + 1))
        ccol[t] = jnp.where(there, rx * REG + (tile & 3), -1000 * (t + 1))

    def near(a, b):
        return (jnp.abs(crow[a] - crow[b]) <= 1) & (jnp.abs(ccol[a] - ccol[b]) <= 1)

    def tile_plan(t, carry):
        plan[t, 0] = (near(t, 0) | near(t, 1)).astype(jnp.int32)
        count = jnp.int32(0)
        for r in range(PAIRS):
            plan[t, 2 + count] = r
            both = jnp.int32(0)
            for s in range(2):
                k = 2 * r + s
                close = near(t, k)
                down, across = crow[k] - crow[t], ccol[k] - ccol[t]
                plan[t, 10 + 8 * s + count] = jnp.where(close, down * 3 + across + 4, FAR)
                plan[t, 26 + 8 * s + count] = jnp.where(
                    close, (64 * down + 8 * across + 512) & 127, 0
                )
                both = both | close.astype(jnp.int32)
            count = count + both
        plan[t, 1] = count
        return carry

    lax.fori_loop(0, TILES, tile_plan, 0)
    plan[0, 47] = my_row & 1


def bias_tables(base_ref, tab):
    query = lax.broadcasted_iota(jnp.int32, (CELLS, 128), 0)
    lane = lax.broadcasted_iota(jnp.int32, (CELLS, 128), 1)
    key = lane & 63
    left = lane < 64
    row_step = (key >> 3) - (query >> 3)
    col_step = (key & 7) - (query & 7)
    base = base_ref[...]
    for place in range(9):
        down, across = place // 3 - 1, place % 3 - 1
        shift = 64 * down + 8 * across
        inside = (jnp.abs(row_step + 8 * down) <= HALO) & (jnp.abs(col_step + 8 * across) <= HALO)
        first = pltpu.roll(base, (-shift - 27) % 128, 1)
        second = pltpu.roll(base, (64 - shift - 27) % 128, 1)
        for h in range(HEADS):
            a = pltpu.roll(
                jnp.broadcast_to(first[h : h + 1], (CELLS, 128)), 0, 1, stride=1, stride_axis=0
            )
            b = pltpu.roll(
                jnp.broadcast_to(second[h : h + 1], (CELLS, 128)), 0, 1, stride=1, stride_axis=0
            )
            tab[place, h * CELLS : (h + 1) * CELLS, :] = jnp.where(
                inside, jnp.where(left, a, b), -jnp.inf
            )
    tab[FAR] = jnp.full((BROWS, 128), -jnp.inf, F32)


def prepare(local, left, right, gain, out):
    normed = out.at[pl.ds(0, PAIRS * ROWS)]
    grads = out.at[pl.ds(PAIRS * ROWS, PAIRS * ROWS)]
    own = out.at[pl.ds(2 * PAIRS * ROWS, ROWS)]
    gain_row = gain[...]

    def norm(block):
        x = block.astype(F32)
        inv = lax.rsqrt(jnp.mean(x * x, axis=-1, keepdims=True) + 1e-06)
        return (x * inv * gain_row).astype(BF)

    own[...] = local[0:ROWS, :]
    for t, source in ((0, local), (6, left), (8, right)):
        at = t * CELLS
        normed[at : at + ROWS, :] = norm(source[0:ROWS, :])
        grads[at : at + ROWS, :] = source[ROWS : 2 * ROWS, :]
    at_a, at_b, at_c = 2 * ROWS, 2 * ROWS + STRIP, 2 * ROWS + 2 * STRIP
    upper = [
        (2, local[at_a : at_a + STRIP, :]),
        (3, local[at_b : at_b + STRIP, :]),
        (10, left[at_a : at_a + STRIP, :]),
        (11, right[at_a : at_a + STRIP, :]),
    ]
    lower = [
        (4, local[at_c : at_c + STRIP, :]),
        (5, local[at_c + STRIP : at_c + 2 * STRIP, :]),
        (12, left[at_b : at_b + STRIP, :]),
        (13, right[at_b : at_b + STRIP, :]),
    ]
    for t, strip in upper:
        at = t * CELLS
        normed[at : at + CELLS - T_ROWS, :] = jnp.zeros((CELLS - T_ROWS, D), BF)
        normed[at + CELLS - T_ROWS : at + CELLS, :] = norm(strip[0:T_ROWS])
        grads[at : at + CELLS - G_ROWS, :] = jnp.zeros((CELLS - G_ROWS, D), BF)
        grads[at + CELLS - G_ROWS : at + CELLS, :] = strip[T_ROWS:STRIP]
    for t, strip in lower:
        at = t * CELLS
        normed[at : at + T_ROWS, :] = norm(strip[0:T_ROWS])
        normed[at + T_ROWS : at + CELLS, :] = jnp.zeros((CELLS - T_ROWS, D), BF)
        grads[at : at + G_ROWS, :] = strip[T_ROWS:STRIP]
        grads[at + G_ROWS : at + CELLS, :] = jnp.zeros((CELLS - G_ROWS, D), BF)


def main_body(
    plan,
    local,
    first,
    second,
    w_mine,
    w_other,
    gain,
    base,
    update,
    grad_tokens,
    sums,
    wq,
    wo,
    qkv,
    gatt,
    qbd,
    gbd,
    scores,
    dprobs,
    top,
    total,
    delta,
    pbf,
    dsf,
    att,
    dq,
    attended,
    dqkv,
    dk,
    dv,
    hist,
    rowsum,
    packed,
    tab,
):
    bias_tables(base, tab)
    prepare(local, first, second, gain, packed)
    normed = packed.at[pl.ds(0, PAIRS * ROWS)]
    grads = packed.at[pl.ds(PAIRS * ROWS, PAIRS * ROWS)]
    tokens = packed.at[pl.ds(2 * PAIRS * ROWS, ROWS)]
    core = plan[0, 47]
    for c, part in ((core, w_mine), (1 - core, w_other)):
        for j in range(3):
            wq[3 * c + j] = part[:, 16 * j : 16 * j + 16, :].reshape(D, 128)
        both = part[:, 48:64, :].astype(F32)
        for j in range(2):
            wo[2 * c + j] = both[:, 8 * j : 8 * j + 8, :].reshape(INNER, 128).astype(BF)

    def columns(blocks, first, last):
        return jnp.concatenate([blocks[j] for j in range(first, last)], axis=1)

    gain_row = gain[...]
    for j in range(3):
        cols = slice(j * INNER, (j + 1) * INNER)
        qkv[:, cols] = dot(normed[...], columns(wq, 2 * j, 2 * j + 2)).astype(BF)
    gatt[...] = dot(grads[...], columns(wo, 0, 4), NT).astype(BF)

    dk[...] = jnp.zeros_like(dk)
    dv[...] = jnp.zeros_like(dv)
    hist[...] = jnp.zeros_like(hist)
    head_of = lax.broadcasted_iota(jnp.int32, (1, INNER), 1) >> 5
    masks_bf = [(head_of == h).astype(F32).astype(BF) for h in range(HEADS)]
    lane = lax.broadcasted_iota(jnp.int32, (CHUNK, 128), 1)
    first_slot = lane < 64
    lane_masks = [((lane[0:CELLS] >> 5) == h).astype(F32) for h in range(4)]
    mirror = ((lane + lax.broadcasted_iota(jnp.int32, (128, 128), 0)) == 127).astype(F32)
    mirror_bf = mirror.astype(BF)

    def process(i, own, q_at, nq):
        per = CHUNK // nq
        chunks = HEADS // per
        used = HEADS * nq
        at = pl.multiple_of(i * CELLS, CELLS) + q_at
        queries = qkv[pl.ds(at, nq), 0:INNER]
        cotangents = gatt[pl.ds(at, nq), :]
        for h in range(HEADS):
            qbd[h * nq : (h + 1) * nq, :] = queries * masks_bf[h]
            gbd[h * nq : (h + 1) * nq, :] = cotangents * masks_bf[h]
        count = plan[i, 1]

        def bias_of(off, c):
            parts = [
                tab[off, (c * per + h) * CELLS + q_at : (c * per + h) * CELLS + q_at + nq, :]
                for h in range(per)
            ]
            return jnp.concatenate(parts, axis=0)

        def pass_a(b, first):
            k_at = pl.multiple_of(plan[i, 2 + b] * ROWS, ROWS)
            keys = qkv[pl.ds(k_at, ROWS), INNER : 2 * INNER]
            values = qkv[pl.ds(k_at, ROWS), 2 * INNER : 3 * INNER]
            off_a, off_b = plan[i, 10 + b], plan[i, 18 + b]
            scores[b, 0:used, :] = dot(qbd[0:used, :], keys, NT)
            dprobs[b, 0:used, :] = dot(gbd[0:used, :], values, NT)
            for c in range(chunks):
                rows = slice(c * CHUNK, (c + 1) * CHUNK)
                bias = jnp.where(first_slot, bias_of(off_a, c), bias_of(off_b, c))
                s = scores[b, rows, :] * SCALE + bias
                scores[b, rows, :] = s
                top[rows, :] = s if first else jnp.maximum(top[rows, :], s)

        def rest_a(b, carry):
            pass_a(b, False)
            return carry

        pass_a(0, True)
        lax.fori_loop(1, count, rest_a, 0)
        for c in range(chunks):
            rows = slice(c * CHUNK, (c + 1) * CHUNK)
            top[rows, :] = jnp.broadcast_to(
                jnp.max(top[rows, :], axis=-1, keepdims=True), (CHUNK, 128)
            )

        def pass_b(b, first):
            for c in range(chunks):
                rows = slice(c * CHUNK, (c + 1) * CHUNK)
                e = jnp.exp(scores[b, rows, :] - top[rows, :])
                d = e * dprobs[b, rows, :]
                scores[b, rows, :] = e
                total[rows, :] = e if first else total[rows, :] + e
                delta[rows, :] = d if first else delta[rows, :] + d

        def rest_b(b, carry):
            pass_b(b, False)
            return carry

        pass_b(0, True)
        lax.fori_loop(1, count, rest_b, 0)
        for c in range(chunks):
            rows = slice(c * CHUNK, (c + 1) * CHUNK)
            inverse = 1.0 / jnp.sum(total[rows, :], axis=-1, keepdims=True)
            d = jnp.sum(delta[rows, :], axis=-1, keepdims=True) * inverse
            total[rows, :] = jnp.broadcast_to(inverse, (CHUNK, 128))
            delta[rows, :] = jnp.broadcast_to(d, (CHUNK, 128))

        def probs_of(b):
            for c in range(chunks):
                rows = slice(c * CHUNK, (c + 1) * CHUNK)
                p = scores[b, rows, :] * total[rows, :]
                pbf[rows, :] = p.astype(BF)
                dsf[rows, :] = (p * (dprobs[b, rows, :] - delta[rows, :])).astype(BF)

        def pass_c(b, first):
            k_at = pl.multiple_of(plan[i, 2 + b] * ROWS, ROWS)
            keys = qkv[pl.ds(k_at, ROWS), INNER : 2 * INNER]
            values = qkv[pl.ds(k_at, ROWS), 2 * INNER : 3 * INNER]
            probs_of(b)
            for sum_ref, factor, other in ((att, pbf, values), (dq, dsf, keys)):
                wide = dot(factor[...], other)
                for n in range(2):
                    cols = slice(n * 128, (n + 1) * 128)
                    acc = None if first else sum_ref[:, cols]
                    for h in range(4 * n, 4 * n + 4):
                        part = wide[h * CELLS : (h + 1) * CELLS, cols] * lane_masks[h & 3]
                        acc = part if acc is None else acc + part
                    sum_ref[:, cols] = acc
            flipped = dot(dsf[...], mirror_bf)
            half = first_slot[0:CELLS]
            for h in range(HEADS):
                ds = flipped[h * CELLS : (h + 1) * CELLS]
                for s, part in enumerate((jnp.where(half, 0.0, ds), jnp.where(half, ds, 0.0))):
                    turned = pltpu.roll(part, 0, 1, stride=1, stride_axis=0)
                    rowsum[s, h : h + 1, :] = jnp.sum(turned, axis=0, keepdims=True)
            for s in range(2):
                shift = (64 * s - 27 - plan[i, 26 + 8 * s + b] + 256) & 127
                hist[...] += pltpu.roll(rowsum[s], shift, 1)

        def rest_c(b, carry):
            pass_c(b, False)
            return carry

        if own:
            pass_c(0, True)
        else:
            probs_of(0)
        dk[...] += dot(dsf[0:used, :], qbd[0:used, :], TN)
        dv[...] += dot(pbf[0:used, :], gbd[0:used, :], TN)
        if own:
            lax.fori_loop(1, count, rest_c, 0)
            slot_at = pl.multiple_of(i * CELLS, CELLS)
            attended[pl.ds(slot_at, CELLS), :] = att[...].astype(BF)
            dqkv[pl.ds(slot_at, CELLS), 0:INNER] = (dq[...] * SCALE).astype(BF)

    def own_step(s, carry):
        process(s, True, 0, CELLS)
        return carry

    lax.fori_loop(0, 2, own_step, 0)

    def others(tile_of, q_at, nq):
        def step(n, carry):
            t = tile_of(n)
            pl.when(plan[t, 0] > 0)(lambda: process(t, False, q_at, nq))
            return carry

        lax.fori_loop(0, 4, step, 0)

    others(lambda n: n + 6, 0, CELLS)
    others(lambda n: n + jnp.where(n < 2, 2, 8), CELLS - G_ROWS, G_ROWS)
    others(lambda n: n + jnp.where(n < 2, 4, 10), 0, G_ROWS)

    dqkv[:, INNER : 2 * INNER] = (dk[...] * SCALE).astype(BF)
    dqkv[:, 2 * INNER : 3 * INNER] = dv[...].astype(BF)
    update[...] = dot(attended[...], columns(wo, 0, 4)).astype(BF)
    grad_out = dot(attended[...], grads[0:ROWS, :], TN)
    for c in range(2):
        pair = [
            grad_out[:, (2 * c + j) * 128 : (2 * c + j + 1) * 128].reshape(DP, 8, 128)
            for j in range(2)
        ]
        both = jnp.concatenate(pair, axis=1).astype(BF)
        for d in range(DP):
            sums[c, d * WROWS + 48 : d * WROWS + 64, :] = both[d]
    for n in range(3):
        pair = dot(normed[0:ROWS, :], dqkv[:, n * 256 : (n + 1) * 256], TN).astype(BF)
        for j in (2 * n, 2 * n + 1):
            block = pair[:, (j - 2 * n) * 128 : (j - 2 * n + 1) * 128]
            for d in range(DP):
                at = d * WROWS + (j % 3) * 16
                sums[j // 3, at : at + 16, :] = block[d * 16 : (d + 1) * 16]
    d_normed = dot(dqkv[...], columns(wq, 0, 6), NT)
    x = tokens[...].astype(F32)
    inv = lax.rsqrt(jnp.mean(x * x, axis=-1, keepdims=True) + 1e-06)
    scaled = d_normed * gain_row
    gain_sum = jnp.sum(d_normed * x * inv, axis=0, keepdims=True)
    grad_tokens[...] = (
        inv * scaled - x * (inv * inv * inv) * jnp.mean(scaled * x, axis=-1, keepdims=True)
    ).astype(BF)
    offsets = lax.dot_general(
        hist[...],
        mirror,
        (((1,), (0,)), ((), ())),
        precision=lax.Precision.HIGHEST,
        preferred_element_type=F32,
    )
    folded = offsets[0:4, :] + pltpu.roll(offsets[4:8, :], 64, 1)
    small = jnp.concatenate([gain_sum[:, j * 128 : (j + 1) * 128] for j in range(4)] + [folded], 0)
    split = halves(small)
    sums[0, DP * WROWS : DP * WROWS + SMALL, :] = split
    sums[1, DP * WROWS : DP * WROWS + SMALL, :] = split


def halves(value):
    high = value.astype(BF).astype(F32)
    return jnp.concatenate([high, value - high], axis=0).astype(BF)


def whole(value):
    wide = value.astype(F32)
    return wide[..., 0:8, :] + wide[..., 8:16, :]


def sum_body(senders, parts, span, received, out):
    rows = parts * span
    for p in range(parts):
        acc = received[0, p * span : (p + 1) * span, :].astype(F32)
        for s in range(1, senders):
            acc += received[s, p * span : (p + 1) * span, :].astype(F32)
        out[p, 0:span, :] = acc.astype(BF)
    small = whole(received[0, rows : rows + SMALL, :])
    for s in range(1, senders):
        small += whole(received[s, rows : rows + SMALL, :])
    split = halves(small)
    for p in range(parts):
        out[p, span : span + SMALL, :] = split


def last_sum_body(received, out):
    acc = received[0, 0:WROWS, :].astype(F32)
    small = whole(received[0, WROWS : WROWS + SMALL, :])
    for s in range(1, DP):
        acc += received[s, 0:WROWS, :].astype(F32)
        small += whole(received[s, WROWS : WROWS + SMALL, :])
    acc = acc.astype(BF)
    split = halves(small)
    for p in range(8):
        out[p, 0:WROWS, :] = acc
        out[p, WROWS : WROWS + SMALL, :] = split


def z_body(received, mine, small):
    acc = received[0, 0:WROWS, :].astype(F32)
    more = whole(received[0, WROWS : WROWS + SMALL, :])
    for s in range(1, 8):
        acc += received[s, 0:WROWS, :].astype(F32)
        more += whole(received[s, WROWS : WROWS + SMALL, :])
    mine[...] = acc.astype(BF)
    small[...] = more


def finish_body(place, mine, theirs, small_in, grad_qkv, grad_out, grad_gain, grad_bias):
    small = small_in[...]
    odd = place[0] & 1

    def unpack(pair):
        for c, ref in enumerate(pair):
            acc = ref[...].astype(F32)
            for j in range(3):
                at = (3 * c + j) * 128
                grad_qkv[:, at : at + 128] = acc[16 * j : 16 * j + 16, :]
            for j in range(2):
                at = 48 + 8 * j
                grad_out[:, (2 * c + j) * 128 : (2 * c + j + 1) * 128] = acc[at : at + 8, :]

    pl.when(odd == 0)(lambda: unpack((mine, theirs)))
    pl.when(odd == 1)(lambda: unpack((theirs, mine)))
    for j in range(4):
        grad_gain[:, j * 128 : (j + 1) * 128] = small[j : j + 1, :]
    folded = small[4:8, :]
    table = jnp.concatenate([folded, pltpu.roll(folded, 64, 1)], axis=0)
    lane = lax.broadcasted_iota(jnp.int32, (HEADS, 128), 1)
    out = jnp.zeros((HEADS, 128), F32)
    for r in range(7):
        moved = table if r == 0 else pltpu.roll(table, 128 - r, 1)
        out = jnp.where((lane >= 7 * r) & (lane < 7 * r + 7), moved, out)
    grad_bias[...] = out[:, 0:49]


def layer(plan, local, first, second, w_mine, w_other, gain, base):
    f32 = lambda *dims: pltpu.VMEM(dims, F32)
    bf = lambda *dims: pltpu.VMEM(dims, BF)
    return call(
        main_body,
        [
            shape((ROWS, D), BF),
            shape((ROWS, D), BF),
            shape((2, DP * WROWS + SMALL, 128), BF),
        ],
        [SM] + [VM] * 7,
        [
            bf(6, D, 128),
            bf(4, INNER, 128),
            bf(PAIRS * ROWS, 3 * INNER),
            bf(PAIRS * ROWS, INNER),
            bf(BROWS, INNER),
            bf(BROWS, INNER),
            f32(4, BROWS, 128),
            f32(4, BROWS, 128),
            f32(BROWS, 128),
            f32(BROWS, 128),
            f32(BROWS, 128),
            bf(BROWS, 128),
            bf(BROWS, 128),
            f32(CELLS, INNER),
            f32(CELLS, INNER),
            bf(ROWS, INNER),
            bf(ROWS, 3 * INNER),
            f32(ROWS, INNER),
            f32(ROWS, INNER),
            f32(HEADS, 128),
            f32(CAP, HEADS, 128),
            bf(2 * PAIRS * ROWS + ROWS, D),
            f32(FAR + 1, BROWS, 128),
        ],
        limit=40,
        flops=4000000000,
        traffic=12000000,
    )(plan, local, first, second, w_mine, w_other, gain, base)


def shards(tokens, tile_ids, w_qkv, w_out, norm_gain, rel_bias, update_grad):
    my_row = lax.axis_index("gy")
    my_col = lax.axis_index("gx")
    place = jnp.stack([my_row, my_col]).astype(jnp.int32)
    pairs = [(0, 1), (1, 0), (2, 3), (3, 2)]
    middle = [(1, 2), (2, 1)]

    tiles = tile_ids.reshape(4, 4, CAP)
    strip = shape((CAP, STRIP, D), BF)
    w_send, rows, near, far = call(
        pack_body,
        [shape((DP, WROWS, 128), BF), shape((2 * ROWS, D), BF), strip, strip],
        [HBM, HBM, HBM, HBM],
        [
            pltpu.VMEM((16, 3 * INNER), BF),
            pltpu.VMEM((8, D), BF),
            pltpu.SemaphoreType.DMA((4,)),
        ],
        limit=60,
    )(w_qkv, w_out, tokens.reshape(ROWS, D), update_grad.reshape(ROWS, D))
    near = lax.ppermute(near, "gy", pairs)
    far = lax.ppermute(far, "gy", middle)
    w_mine = lax.all_to_all(w_send, "dp", 0, 0, tiled=True)
    message = shape((MESSAGE, D), BF)
    stays = shape((2 * ROWS + 4 * STRIP, D), BF)
    first, second, local = call(
        corner_body, [message, message, stays], [SM, SM, VM, VM, VM], flops=16000000000
    )(place, tiles, rows, near, far)
    first = lax.ppermute(first, "gx", pairs)
    second = lax.ppermute(second, "gx", middle)
    base = jnp.pad(rel_bias.reshape(HEADS, 7, 7), ((0, 0), (0, 0), (0, 1))).reshape(HEADS, 56)
    base = jnp.pad(base, ((0, 0), (0, 72)))
    plan = pl.pallas_call(
        plan_tiles,
        out_shape=shape((TILES, 48), jnp.int32),
        in_specs=[SM, SM],
        out_specs=SM,
        scratch_shapes=[pltpu.SMEM((TILES,), jnp.int32), pltpu.SMEM((TILES,), jnp.int32)],
        cost_estimate=pl.CostEstimate(flops=2000000, bytes_accessed=4000000, transcendentals=0),
    )(place, tiles)
    w_mine = lax.optimization_barrier((w_mine, first, second, plan))[0]
    w_other = lax.ppermute(w_mine, "gy", pairs)

    update, grad_tokens, sums = layer(
        plan, local, first, second, w_mine, w_other, norm_gain.reshape(1, D), base
    )

    got = lax.all_to_all(sums, "gy", 0, 0, tiled=True, axis_index_groups=CORES)
    got = call(
        functools.partial(sum_body, 2, DP, WROWS), shape((DP, WROWS + SMALL, 128), BF), [VM]
    )(got)
    got = lax.all_to_all(got, "dp", 0, 0, tiled=True)
    got = call(last_sum_body, shape((8, WROWS + SMALL, 128), BF), [VM])(got)
    got = lax.all_to_all(got, ("gy", "gx"), 0, 0, tiled=True, axis_index_groups=ZS)
    mine, small = call(z_body, [shape((WROWS, 128), BF), shape((8, 128), F32)], [VM])(got)
    theirs = lax.ppermute(mine, "gy", pairs)
    grad_qkv, grad_out, grad_gain, grad_bias = call(
        finish_body,
        [
            shape((16, 3 * INNER), F32),
            shape((8, D), F32),
            shape((1, D), F32),
            shape((HEADS, 49), F32),
        ],
        [SM, VM, VM, VM],
    )(place, mine, theirs, small)
    return (
        update.reshape(tokens.shape),
        grad_tokens.reshape(tokens.shape),
        grad_qkv,
        grad_out,
        grad_gain.reshape(D),
        grad_bias,
    )


def solution(mesh):
    return jax.shard_map(
        shards,
        mesh=mesh,
        in_specs=(
            P("dp", "gy", "gx", None, None),
            P("dp", None, None, None),
            P("dp", None),
            P("dp", None),
            P(),
            P(),
            P("dp", "gy", "gx", None, None),
        ),
        out_specs=(
            P("dp", "gy", "gx", None, None),
            P("dp", "gy", "gx", None, None),
            P("dp", None),
            P("dp", None),
            P(),
            P(),
        ),
        check_vma=False,
    )
```
